128 devices in a mesh: row: 4 (over z), col: 8 (over x_hi, y), tp: 4 (over x_lo, core).
Axes of the slice: x: 4 (x_hi: 2, x_lo: 2; x = x_hi * 2 + x_lo), y: 4, z: 4, core: 2. Of those that a mesh axis runs over, the one named last changes fastest.
Arguments:
- tokens: bfloat16 [32, 128, 3200], P('row', 'col', 'tp'), may hold values from -6 to 6
- cotangent: bfloat16 [32, 128, 3200], P('row', 'col', 'tp'), may hold values from -6 to 6
- expand_weight: bfloat16 [3200, 6400], P(None, 'tp'), may hold values from -0.10606602 to 0.10606602
- reduce_weight: bfloat16 [3200, 6400], P(None, 'tp'), may hold values from -0.075 to 0.075
- position_kernel: float32 [3, 3, 3200], replicated, may hold values from -1.5 to 1.5
- norm_gain: float32 [3200], replicated, may hold values from 0.2 to 2.4
Outputs:
- grad_tokens: bfloat16 [32, 128, 3200], P('row', 'col', 'tp')
- grad_expand: float32 [3200, 6400], P(('row', 'col'), 'tp')
- grad_reduce: float32 [3200, 6400], P(('row', 'col'), 'tp')
- grad_kernel: float32 [3, 3, 3200], P(None, None, 'tp')
- grad_gain: float32 [3200], P('tp')
The draws below stay inside these ranges and needn't reach their ends.
All inputs are finite; a program needn't handle non-finite values.
Results may differ from the reference program's by a relative error of at most 0.029.
Values may be sent and summed in bfloat16 or wider, within the bound.
A program may use at most 192 MiB of HBM per device.

```python
import jax
import jax.numpy as jnp
from jax import lax

D = 3200
H = 6400
R_DEV = 8
C_DEV = 16
GR = 32
GC = 128
TOKENS = 4096
N_ROW = 4
N_COL = 8


feature_groups = 16


def token_pair(key):
    first_key = jax.random.fold_in(key, 101)
    second_key = jax.random.fold_in(key, 102)
    sign_key = jax.random.fold_in(key, 104)
    group_width = D // feature_groups
    base = jax.random.normal(first_key, (GR, GC, D), jnp.float32)
    noise = jax.random.normal(second_key, (GR, GC, D), jnp.float32)
    group_signs = 2.0 * jax.random.bernoulli(sign_key, 0.5, (GR, GC, feature_groups)).astype(jnp.float32) - 1.0
    signs = jnp.repeat(group_signs, group_width, axis=2)
    inputs = jnp.clip(base, -6.0, 6.0)
    upstream = jnp.clip(0.9 * signs * inputs + 0.44 * noise, -6.0, 6.0)
    return (inputs, upstream)


def weight_pair(key):
    shared = jnp.clip(jax.random.normal(jax.random.fold_in(key, 201), (D, H), jnp.float32), -6.0, 6.0)
    noise = jax.random.normal(jax.random.fold_in(key, 202), (D, H), jnp.float32)
    first = shared * D ** (-0.5)
    second = jnp.clip(0.8 * shared + 0.6 * noise, -6.0, 6.0) * H ** (-0.5)
    return (first, second)


def draw_tokens(key, part):
    return token_pair(key)[0].astype(jnp.bfloat16)


def draw_cotangent(key, part):
    return token_pair(key)[1].astype(jnp.bfloat16)


def draw_expand_weight(key, part):
    return weight_pair(key)[0].astype(jnp.bfloat16)


def draw_reduce_weight(key, part):
    return weight_pair(key)[1].astype(jnp.bfloat16)


def draw_norm_gain(key, part):
    ramp = 0.3 + 1.4 * (jnp.arange(D, dtype=jnp.float32) + 0.5) / D
    spread = jax.random.uniform(jax.random.fold_in(key, 301), (D,), jnp.float32, 0.7, 1.4)
    return ramp * spread


def bell_draw(own_key, extent, deviation, limit, kind=jnp.bfloat16):
    return jnp.clip(deviation * jax.random.normal(own_key, extent, jnp.float32), -limit, limit).astype(kind)


def setup_inputs(seed: int = 0) -> dict:
    key_of = jax.random.split(jax.random.key(seed), 7)
    return {
        "tokens": draw_tokens(jax.random.fold_in(key_of[6], 71), 0),
        "cotangent": draw_cotangent(jax.random.fold_in(key_of[6], 71), 0),
        "expand_weight": draw_expand_weight(jax.random.fold_in(key_of[6], 71), 0),
        "reduce_weight": draw_reduce_weight(jax.random.fold_in(key_of[6], 71), 0),
        "position_kernel": bell_draw(key_of[4], (3, 3, D), 0.3, 1.5, jnp.float32),
        "norm_gain": draw_norm_gain(jax.random.fold_in(key_of[6], 71), 0),
    }


epsilon = 1e-06

def depthwise(field, kernel):
    row_cells, col_cells = (field.shape[0], field.shape[1])
    padded = jnp.pad(field, ((1, 1), (1, 1), (0, 0)))
    summed = jnp.zeros(field.shape, jnp.float32)
    for row_shift in range(3):
        for col_shift in range(3):
            summed = summed + kernel[row_shift, col_shift] * padded[row_shift:row_shift + row_cells, col_shift:col_shift + col_cells]
    return summed

def transposed(field, kernel):
    row_cells, col_cells = (field.shape[0], field.shape[1])
    padded = jnp.pad(field, ((1, 1), (1, 1), (0, 0)))
    summed = jnp.zeros(field.shape, jnp.float32)
    for row_shift in range(3):
        for col_shift in range(3):
            summed = summed + kernel[row_shift, col_shift] * padded[2 - row_shift:2 - row_shift + row_cells, 2 - col_shift:2 - col_shift + col_cells]
    return summed

def kernel_grad(grad_field, field):
    row_cells, col_cells = (field.shape[0], field.shape[1])
    padded = jnp.pad(field, ((1, 1), (1, 1), (0, 0)))
    pieces = []
    for row_shift in range(3):
        for col_shift in range(3):
            pieces.append(lax.optimization_barrier(jnp.sum(grad_field * padded[row_shift:row_shift + row_cells, col_shift:col_shift + col_cells], axis=(0, 1))))
    return jnp.stack(pieces).reshape(3, 3, field.shape[2])

def gelu_slope(pre_act):
    cdf = 0.5 * (1.0 + lax.erf(pre_act * 0.7071067811865476))
    density = jnp.exp(-0.5 * pre_act * pre_act) * 0.3989422804014327
    return cdf + pre_act * density

def regroup(flat, columns):
    blocks = flat.reshape(N_ROW, R_DEV, N_COL, C_DEV, columns).transpose(0, 2, 1, 3, 4)
    return blocks.reshape(N_ROW * N_COL, R_DEV * C_DEV, columns)

def reference(tokens, cotangent, expand_weight, reduce_weight, position_kernel, norm_gain):
    x_float = tokens.astype(jnp.float32)
    positioned = (x_float + depthwise(x_float, position_kernel)).astype(jnp.bfloat16)
    h_float = positioned.astype(jnp.float32)
    inverse = lax.rsqrt(lax.optimization_barrier(jnp.mean(h_float * h_float, axis=-1, keepdims=True)) + epsilon)
    normed = (h_float * inverse * norm_gain).astype(jnp.bfloat16)
    flat_norm = normed.reshape(TOKENS, D)
    flat_cot = cotangent.reshape(TOKENS, D)
    pre_act = jnp.dot(flat_norm, expand_weight, preferred_element_type=jnp.float32)
    activated = jax.nn.gelu(pre_act, approximate=False).astype(jnp.bfloat16)
    d_act = jnp.dot(flat_cot, reduce_weight, preferred_element_type=jnp.float32)
    d_pre = (d_act * gelu_slope(pre_act)).astype(jnp.bfloat16)
    d_norm = lax.dot_general(d_pre, expand_weight, (((1,), (1,)), ((), ())), preferred_element_type=jnp.float32)
    d_norm = d_norm.reshape(GR, GC, D)
    scaled = d_norm * norm_gain
    inner_dot = lax.optimization_barrier(jnp.sum(scaled * h_float, axis=-1, keepdims=True))
    d_mlp = inverse * scaled - h_float * inverse ** 3 * inner_dot / D
    d_hidden = (cotangent.astype(jnp.float32) + d_mlp).astype(jnp.bfloat16)
    dh_float = d_hidden.astype(jnp.float32)
    grad_tokens = (dh_float + transposed(dh_float, position_kernel)).astype(jnp.bfloat16)
    factor = TOKENS ** (-0.5)
    grad_gain = lax.optimization_barrier(jnp.sum(d_norm * h_float * inverse, axis=(0, 1))) * factor
    grad_kernel = kernel_grad(dh_float, x_float) * factor
    grouped = (regroup(flat_norm, D), regroup(d_pre, H), regroup(flat_cot, D), regroup(activated, H))

    def accumulate(carry, group):
        norm_block, pre_block, cot_block, act_block = group
        first = lax.dot_general(norm_block, pre_block, (((0,), (0,)), ((), ())), preferred_element_type=jnp.float32) * factor
        second = lax.dot_general(cot_block, act_block, (((0,), (0,)), ((), ())), preferred_element_type=jnp.float32) * factor
        first_round = lax.optimization_barrier(first.astype(jnp.bfloat16))
        second_round = lax.optimization_barrier(second.astype(jnp.bfloat16))
        return ((carry[0] + first_round.astype(jnp.float32), carry[1] + second_round.astype(jnp.float32)), None)
    start_sums = (jnp.zeros((D, H), jnp.float32), jnp.zeros((D, H), jnp.float32))
    sums, unused = lax.scan(accumulate, start_sums, grouped)
    return (grad_tokens, sums[0], sums[1], grad_kernel, grad_gain)
```

```python
import jax
import jax.numpy as jnp
from jax import lax
from jax.experimental import pallas as pl
from jax.experimental.pallas import tpu as pltpu
from jax.sharding import PartitionSpec as P

MESH = pl.DeviceIdType.MESH
F32 = jnp.float32
BF16 = jnp.bfloat16
epsilon = 1e-06
ROWS, COLS, TOK = 8, 16, 128
DQ, D = 800, 3200
HD, HP, HQ = 1600, 1664, 400
NT = (((1,), (1,)), ((), ()))


def mul(value, by):
    return pl.multiple_of(value, by)


def kernel(
    tok_ref, cot_ref, w1_hbm, w2_hbm, pk_ref, gain_ref,
    gt_ref, ge_ref, gr_ref, kg_ref,
    w1, w2, padded, padded2, cot, pos, trans, pre, dact, inv, bt, b1, at, btile,
    e_send, e_recv, inn, erow, ecol, rrow, rcol, rcor, xs, xr, keep, ys, yr, kall,
    send_sem, recv_sem, local_sem, wsem,
):
    z = lax.axis_index("row")
    col = lax.axis_index("col")
    tp = lax.axis_index("tp")
    xh, y = col // 4, col % 4
    xl, core = tp // 2, tp % 2

    def at_y(d):
        return (z, xh * 4 + (y + d) % 4, tp)

    def at_z(d):
        return ((z + d) % 4, col, tp)

    def at_grid(dr, dc):
        return ((z + dr + 4) % 4, (col + dc + 8) % 8, tp)

    x_peer = (z, (1 - xh) * 4 + y, tp)
    tp_sib = xl * 2 + 1 - core
    tp_cross = (1 - xl) * 2 + core
    tp_far = (1 - xl) * 2 + 1 - core
    sib, cross, far = (z, col, tp_sib), (z, col, tp_cross), (z, col, tp_far)

    grid_steps = [(1, 0), (-1, 0), (0, 1), (0, -1), (1, 1), (1, -1), (-1, 1), (-1, -1)]
    peers = [at_grid(*s) for s in grid_steps]
    peers += [at_y(d) for d in (1, 2, 3)] + [at_z(d) for d in (1, 2, 3)]
    peers += [x_peer, sib, cross, far]
    barrier = pltpu.get_barrier_semaphore()
    for peer in peers:
        pl.semaphore_signal(barrier, inc=1, device_id=peer, device_id_type=MESH)

    counts = {"remote": 0, "local": 0}
    started = []

    def send(src, dst, to):
        k = counts["remote"]
        counts["remote"] += 1
        copy = pltpu.make_async_remote_copy(
            src_ref=src, dst_ref=dst, send_sem=send_sem.at[k], recv_sem=recv_sem.at[k],
            device_id=to, device_id_type=MESH,
        )
        copy.start()
        started.append(copy)
        return copy

    def local(src, dst):
        k = counts["local"]
        counts["local"] += 1
        copy = pltpu.make_async_copy(src, dst, local_sem.at[k])
        copy.start()
        return copy

    def arrived(copies):
        for copy in copies:
            copy.wait_recv()

    order = [tp, tp_sib, tp_cross, tp_far]
    w_copies = []
    for n, (src, dst) in enumerate(((w2_hbm, w2), (w1_hbm, w1))):
        for k, j in enumerate(order):
            rows = pl.ds(mul(j * DQ, 16), DQ)
            copy = pltpu.make_async_copy(src.at[rows], dst.at[rows], wsem.at[n * 4 + k])
            copy.start()
            w_copies.append(copy)

    def fill_edges(field, n):
        erow[n, 0] = field[1, 8:24, :]
        erow[n, 1] = field[8, 8:24, :]
        for i in range(ROWS):
            ecol[n, 0, i : i + 1, :] = field[i + 1, 8:9, :]
            ecol[n, 1, i : i + 1, :] = field[i + 1, 23:24, :]

    def send_edges(n):
        low, high = pl.ds(0, 8), pl.ds(8, 8)
        return [
            send(erow.at[n, 1], rrow.at[n, 0], at_grid(1, 0)),
            send(erow.at[n, 0], rrow.at[n, 1], at_grid(-1, 0)),
            send(ecol.at[n, 1], rcol.at[n, 0], at_grid(0, 1)),
            send(ecol.at[n, 0], rcol.at[n, 1], at_grid(0, -1)),
            send(erow.at[n, 1, high], rcor.at[n, 0], at_grid(1, 1)),
            send(erow.at[n, 1, low], rcor.at[n, 1], at_grid(1, -1)),
            send(erow.at[n, 0, high], rcor.at[n, 2], at_grid(-1, 1)),
            send(erow.at[n, 0, low], rcor.at[n, 3], at_grid(-1, -1)),
        ]

    one, zero = jnp.float32(1), jnp.float32(0)
    top = jnp.where(z > 0, one, zero)
    bottom = jnp.where(z < 3, one, zero)
    left = jnp.where(col > 0, one, zero)
    right = jnp.where(col < 7, one, zero)

    def fill_halo(field, n):
        field[0, 8:24, :] = rrow[n, 0] * top
        field[9, 8:24, :] = rrow[n, 1] * bottom
        for i in range(ROWS):
            field[i + 1, 7:8, :] = rcol[n, 0, i : i + 1, :] * left
            field[i + 1, 24:25, :] = rcol[n, 1, i : i + 1, :] * right
        field[0, 7:8, :] = rcor[n, 0, 7:8, :] * (top * left)
        field[0, 24:25, :] = rcor[n, 1, 0:1, :] * (top * right)
        field[9, 7:8, :] = rcor[n, 2, 7:8, :] * (bottom * left)
        field[9, 24:25, :] = rcor[n, 3, 0:1, :] * (bottom * right)

    for i in range(ROWS):
        padded[i + 1, 8:24, :] = tok_ref[i].astype(F32)
        cot[tp, i * COLS : (i + 1) * COLS, 0:DQ] = cot_ref[i]
    fill_edges(padded, 0)
    pl.semaphore_wait(barrier, len(peers))
    halo = send_edges(0)
    cot_sib = send(cot.at[tp], cot.at[tp], sib)
    cot_cross = send(cot.at[tp], cot.at[tp], cross)
    pre[:, 1536:1664] = jnp.zeros((TOK, 128), F32)
    dact[:, 1536:1664] = jnp.zeros((TOK, 128), F32)

    arrived(halo)
    fill_halo(padded, 0)

    def conv_row(i, carry):
        total = padded[i + 1, 8:24, :]
        for p in range(3):
            for q in range(3):
                total = total + pk_ref[tp, p * 3 + q : p * 3 + q + 1, :] * padded[i + p, 7 + q : 23 + q, :]
        pos[tp, pl.ds(mul(i * COLS, 16), COLS), 0:DQ] = total.astype(BF16)
        return carry

    lax.fori_loop(0, ROWS, conv_row, 0)
    pos_cross = send(pos.at[tp], pos.at[tp], cross)
    pos_sib = send(pos.at[tp], pos.at[tp], sib)

    def transpose_chunk(g, j, scale):
        source = pos if g else cot

        def tile(k, carry):
            lanes = pl.ds(mul(k * 128, 128), 128)
            part = source[j, :, lanes].astype(F32)
            if scale:
                part = part * gain_ref[j, 0:1, lanes]
            trans[g, j, lanes, :] = part.T.astype(BF16)
            return carry

        lax.fori_loop(0, 7, tile, 0)

    def act_chunk(k):
        j = order[k]
        w_copies[k].wait()
        part = jnp.dot(cot[j, :, 0:DQ], w2[pl.ds(mul(j * DQ, 16), DQ), :], preferred_element_type=F32)
        dact[:, 0:HD] = part if k == 0 else dact[:, 0:HD] + part
        transpose_chunk(0, j, False)

    def pre_chunk(k):
        j = order[k]
        w_copies[4 + k].wait()
        value = pos[j, :, 0:DQ].astype(F32)
        squares = jnp.sum(value * value, axis=1, keepdims=True)
        scaled = (value * gain_ref[j, 0:1, 0:DQ]).astype(BF16)
        part = jnp.dot(scaled, w1[pl.ds(mul(j * DQ, 16), DQ), :], preferred_element_type=F32)
        pre[:, 0:HD] = part if k == 0 else pre[:, 0:HD] + part
        transpose_chunk(1, j, True)
        return squares

    arrived([cot_cross])
    cot_far = send(cot.at[tp_cross], cot.at[tp_cross], sib)
    act_chunk(0)
    arrived([cot_sib])
    act_chunk(1)
    act_chunk(2)
    arrived([pos_cross])
    pos_far = send(pos.at[tp_cross], pos.at[tp_cross], sib)
    arrived([cot_far])
    act_chunk(3)

    own_half = pl.ds(mul(core * HQ, 16), HQ)

    def lanes_of(z_index):
        return pl.ds(mul(z_index * TOK, 128), TOK)

    def spread_a(g):
        copies = []
        for d in (1, 2, 3):
            target = (z + d) % 4
            copies.append(send(trans.at[g, target, own_half], at.at[g, y, own_half, lanes_of(z)], at_z(d)))
        own = local(trans.at[g, z, own_half], at.at[g, y, own_half, lanes_of(z)])
        return copies, own

    def spread_b(g):
        copies = []
        for d in (1, 2, 3):
            target = (y + d) % 4
            rows = pl.ds(mul(target * HQ, 16), HQ)
            copies.append(send(bt.at[g, rows], btile.at[g, y, :, lanes_of(z)], at_y(d)))
        rows = pl.ds(mul(y * HQ, 16), HQ)
        own = local(bt.at[g, rows], btile.at[g, y, :, lanes_of(z)])
        return copies, own

    def gather_a(g, spread):
        arrived(spread[0])
        spread[1].wait()
        block = at.at[g, y, own_half]
        copies = [send(block, block, at_y(d)) for d in (1, 3, 2)]
        return copies, [send(block, block, sib)]

    def share_a(g, gathered):
        for d, copy in zip((1, 3, 2), gathered[0]):
            copy.wait_recv()
            block = at.at[g, (y - d + 4) % 4, own_half]
            gathered[1].append(send(block, block, sib))

    def gather_b(g, spread):
        arrived(spread[0])
        spread[1].wait()
        block = btile.at[g, :, :, lanes_of(z)]
        return [send(block, block, at_z(d)) for d in (1, 3, 2)]

    spread_cot = spread_a(0)
    squares = pre_chunk(0)
    arrived([pos_sib])
    squares = squares + pre_chunk(1)
    squares = squares + pre_chunk(2)
    gather_cot = gather_a(0, spread_cot)
    arrived([pos_far])
    squares = squares + pre_chunk(3)
    inv[...] = jnp.broadcast_to(lax.rsqrt(squares * (1.0 / D) + epsilon), (TOK, 128))

    spread_pos = spread_a(1)

    def gelu_tile(k, total):
        lanes = pl.ds(mul(k * 128, 128), 128)
        raw = pre[:, lanes]
        scale = inv[...]
        value = raw * scale
        cdf = 0.5 * (1.0 + lax.erf(value * 0.7071067811865476))
        density = jnp.exp(-0.5 * value * value) * 0.3989422804014327
        slope = (dact[:, lanes] * (cdf + value * density) * scale).astype(BF16)
        b1[:, lanes] = slope
        slope = slope.astype(F32)
        bt[0, lanes, :] = (value * cdf).T.astype(BF16)
        bt[1, lanes, :] = slope.T.astype(BF16)
        return total + slope * raw

    inner = lax.fori_loop(0, 13, gelu_tile, jnp.zeros((TOK, 128), F32))
    spread_act = spread_b(0)
    spread_pre = spread_b(1)
    inn[tp] = jnp.broadcast_to(jnp.sum(inner.T, axis=0, keepdims=True), (8, 128))
    inner_copies = [send(inn.at[tp], inn.at[tp], to) for to in (sib, cross, far)]

    def norm_chunk(j):
        part = lax.dot_general(
            b1[:, 0:HD], w1[pl.ds(mul(j * DQ, 16), DQ), :], NT, preferred_element_type=F32
        )
        return part.astype(BF16)

    e_copies = []
    for k, (j, to) in enumerate(((tp_far, far), (tp_cross, cross), (tp_sib, sib))):
        e_send[k] = norm_chunk(j)
        e_copies.append(send(e_send.at[k], e_recv.at[tp], to))
        if k == 0:
            gather_act = gather_b(0, spread_act)
        if k == 1:
            gather_pre = gather_b(1, spread_pre)
    e_recv[tp] = norm_chunk(tp)
    gather_pos = gather_a(1, spread_pos)
    share_a(0, gather_cot)

    arrived(inner_copies)
    arrived(e_copies)
    inner_row = inn[0] + inn[1] + inn[2] + inn[3]
    factor = inv[...] * inv[...] * (1.0 / D)
    inv[...] = jnp.broadcast_to(inner_row[0:1, :], (TOK, 128)).T * factor

    def hidden_row(i, total):
        rows = pl.ds(mul(i * COLS, 16), COLS)
        e = e_recv[0, rows, :].astype(F32) + e_recv[1, rows, :].astype(F32)
        e = e + e_recv[2, rows, :].astype(F32) + e_recv[3, rows, :].astype(F32)
        h = pos[tp, rows, 0:DQ].astype(F32)
        d = cot[tp, rows, 0:DQ].astype(F32) + gain_ref[tp, 0:1, 0:DQ] * e - h * inv[rows, 0:1]
        padded2[i + 1, 8:24, :] = d.astype(BF16).astype(F32)
        return total + e * h

    gain_sum = lax.fori_loop(0, ROWS, hidden_row, jnp.zeros((COLS, DQ), F32))
    fill_edges(padded2, 1)
    halo2 = send_edges(1)

    kall[0, y] = jnp.zeros((16, DQ), F32)
    kall[0, y, 9:10, :] = jnp.sum(gain_sum, axis=0, keepdims=True)
    for n in range(7):
        lanes = slice(n * 128, min(n * 128 + 128, DQ))
        width = lanes.stop - lanes.start

        def taps(i, totals, lanes=lanes):
            d = padded2[i + 1, 8:24, lanes]
            return tuple(
                totals[p * 3 + q] + d * padded[i + p, 7 + q : 23 + q, lanes] for p in range(3) for q in range(3)
            )

        sums = lax.fori_loop(0, ROWS, taps, tuple(jnp.zeros((COLS, width), F32) for _ in range(9)))
        for k in range(9):
            kall[0, y, k : k + 1, lanes] = jnp.sum(sums[k], axis=0, keepdims=True)
    k_copies = [send(kall.at[0, y], kall.at[0, y], at_y(d)) for d in (1, 2, 3)]

    arrived(halo2)
    fill_halo(padded2, 1)

    def back_row(i, carry):
        total = padded2[i + 1, 8:24, :]
        for p in range(3):
            for q in range(3):
                total = total + pk_ref[tp, p * 3 + q : p * 3 + q + 1, :] * padded2[i + 2 - p, 9 - q : 25 - q, :]
        gt_ref[i] = total.astype(BF16)
        return carry

    lax.fori_loop(0, ROWS, back_row, 0)
    arrived(k_copies)
    kall[1, z] = kall[0, 0] + kall[0, 1] + kall[0, 2] + kall[0, 3]
    k_copies = [send(kall.at[1, z], kall.at[1, z], at_z(d)) for d in (1, 2, 3)]

    s = float(TOK * 32) ** -0.5

    def half(g, which):
        rows = pl.ds(mul(which * HQ, 16), HQ)
        total = lax.dot_general(at[g, 0, rows, :], btile[g, 0], NT, preferred_element_type=F32)
        for k in range(1, 4):
            total = total + lax.dot_general(at[g, k, rows, :], btile[g, k], NT, preferred_element_type=F32)
        return total * s

    def product(g, gathered_a, gathered_b):
        arrived(gathered_a[1])
        arrived(gathered_b)
        xs[g] = half(g, 1 - xh).astype(BF16)
        copy = send(xs.at[g], xr.at[g], x_peer)
        keep[g] = half(g, xh)
        return copy

    def turn(g, copy):
        copy.wait_recv()
        for k in range(4):
            rows = slice(k * 100, k * 100 + 100)
            ys[g, k, 0:100, :] = (keep[g, rows, :] + xr[g, rows, :].astype(F32)).astype(BF16)
        own = local(ys.at[g, y], yr.at[g, y])
        return [send(ys.at[g, (y + d) % 4], yr.at[g, y], at_y(d)) for d in (1, 3, 2)], own

    def finish(g, turned, out_ref):
        arrived(turned[0])
        turned[1].wait()
        for k in range(4):
            out_ref[:, k * HQ : (k + 1) * HQ] = yr[g, k, 0:100, :].astype(F32)

    x_copy0 = product(0, gather_cot, gather_act)
    arrived(k_copies)
    kall[2, xh] = kall[1, 0] + kall[1, 1] + kall[1, 2] + kall[1, 3]
    k_copy = send(kall.at[2, xh], kall.at[2, xh], x_peer)
    share_a(1, gather_pos)
    turn0 = turn(0, x_copy0)
    arrived([k_copy])
    kg_ref[...] = (kall[2, 0] + kall[2, 1]) * s
    x_copy1 = product(1, gather_pos, gather_pre)
    finish(0, turn0, gr_ref)
    turn1 = turn(1, x_copy1)
    finish(1, turn1, ge_ref)
    for copy in started:
        copy.wait_send()


def on_device(tokens, cotangent, expand_weight, reduce_weight, position_kernel, norm_gain):
    kernels = position_kernel.reshape(9, 4, DQ).transpose(1, 0, 2)
    gains = jnp.pad(norm_gain.reshape(4, 1, DQ), ((0, 0), (0, 0), (0, 96)))
    vmem = pl.BlockSpec(memory_space=pltpu.VMEM)
    hbm = pl.BlockSpec(memory_space=pl.ANY)
    f32, bf16 = (lambda *s: pltpu.VMEM(s, F32)), (lambda *s: pltpu.VMEM(s, BF16))
    grad_tokens, grad_expand, grad_reduce, small = pl.pallas_call(
        kernel,
        out_shape=(
            jax.ShapeDtypeStruct((ROWS, COLS, DQ), BF16),
            jax.ShapeDtypeStruct((100, HD), F32),
            jax.ShapeDtypeStruct((100, HD), F32),
            jax.ShapeDtypeStruct((16, DQ), F32),
        ),
        in_specs=[vmem, vmem, hbm, hbm, vmem, vmem],
        out_specs=(vmem, vmem, vmem, vmem),
        scratch_shapes=[
            bf16(D, HD), bf16(D, HD),
            f32(10, 32, DQ), f32(10, 32, DQ),
            bf16(4, TOK, 896), bf16(4, TOK, 896),
            bf16(2, 4, 896, TOK),
            f32(TOK, HP), f32(TOK, HP),
            f32(TOK, 128),
            bf16(2, HP, TOK), bf16(TOK, HP),
            bf16(2, 4, DQ, 512), bf16(2, 4, HQ, 512),
            bf16(3, TOK, DQ), bf16(4, TOK, DQ),
            f32(4, 8, 128),
            f32(2, 2, 16, DQ), f32(2, 2, 8, DQ),
            f32(2, 2, 16, DQ), f32(2, 2, 8, DQ), f32(2, 4, 8, DQ),
            bf16(2, HQ, HQ), bf16(2, HQ, HQ), f32(2, HQ, HQ),
            bf16(2, 4, 112, HQ), bf16(2, 4, 112, HQ),
            f32(3, 4, 16, DQ),
            pltpu.SemaphoreType.DMA((96,)), pltpu.SemaphoreType.DMA((96,)),
            pltpu.SemaphoreType.DMA((8,)), pltpu.SemaphoreType.DMA((8,)),
        ],
        compiler_params=pltpu.CompilerParams(
            collective_id=0, has_side_effects=True, vmem_limit_bytes=60 * 2**20
        ),
        name="mlp_backward",
    )(tokens, cotangent, expand_weight, reduce_weight, kernels, gains)
    return grad_tokens, grad_expand, grad_reduce, small[0:9].reshape(3, 3, DQ), small[9]


def solution(mesh):
    placed = (P("row", "col", "tp"), P("row", "col", "tp"), P(None, "tp"), P(None, "tp"), P(), P())
    return jax.shard_map(
        on_device,
        mesh=mesh,
        in_specs=placed,
        out_specs=(
            P("row", "col", "tp"),
            P(("row", "col"), "tp"),
            P(("row", "col"), "tp"),
            P(None, None, "tp"),
            P("tp"),
        ),
        check_vma=False,
    )
```

```python
import jax
import jax.numpy as jnp
from jax import lax
from jax.experimental import pallas as pl
from jax.experimental.pallas import tpu as pltpu
from jax.sharding import PartitionSpec as P

MESH = pl.DeviceIdType.MESH
F32 = jnp.float32
BF16 = jnp.bfloat16
epsilon = 1e-06
ROWS, COLS, TOK = 8, 16, 128
DQ, D, FR = 800, 3200, 896
HD, HQ = 1600, 400
NT = (((1,), (1,)), ((), ()))
PARTS = ((0, 0, 400), (1, 0, 256), (1, 256, 144))


def mul(value, by):
    return pl.multiple_of(value, by)


def kernel(
    tok_ref, cot_ref, w1_hbm, w2_hbm, pk_ref, gain_ref,
    gt_ref, yr0, yr1, yr2, kg_ref,
    w1, w2, padded, padded2, cot, pos, trans, pre, dact, inv, bt, b1, at, btile,
    e_send, e_recv, inn, erow, ecol, rrow, rcol, rcor,
    xs0, xs1, xs2, xr0, xr1, xr2, keep0, keep1, keep2, ys0, ys1, ys2, kall,
    send_sem, recv_sem, local_sem, wsem,
):
    z = lax.axis_index("row")
    col = lax.axis_index("col")
    tp = lax.axis_index("tp")
    xh, y = col // 4, col % 4
    xl, core = tp // 2, tp % 2

    def at_y(d):
        return (z, xh * 4 + (y + d) % 4, tp)

    def at_z(d):
        return ((z + d) % 4, col, tp)

    def at_grid(dr, dc):
        return ((z + dr + 4) % 4, (col + dc + 8) % 8, tp)

    x_peer = (z, (1 - xh) * 4 + y, tp)
    tp_sib = xl * 2 + 1 - core
    tp_cross = (1 - xl) * 2 + core
    tp_far = (1 - xl) * 2 + 1 - core
    sib, cross, far = (z, col, tp_sib), (z, col, tp_cross), (z, col, tp_far)

    w_copies = []
    for n, (src, dst) in enumerate(((w2_hbm, w2), (w1_hbm, w1))):
        for k in range(4):
            rows = pl.ds(k * HQ, HQ)
            copy = pltpu.make_async_copy(src.at[rows], dst.at[rows], wsem.at[n * 4 + k])
            copy.start()
            w_copies.append(copy)

    for g in range(2):
        for j in range(4):
            trans[g, j, 0:96, :] = jnp.zeros((96, TOK), BF16)
            trans[g, j, 800:896, :] = jnp.zeros((96, TOK), BF16)

    grid_steps = [(1, 0), (-1, 0), (0, 1), (0, -1), (1, 1), (1, -1), (-1, 1), (-1, -1)]
    peers = [at_grid(*s) for s in grid_steps]
    peers += [at_y(d) for d in (1, 2, 3)] + [at_z(d) for d in (1, 2, 3)]
    peers += [x_peer, sib, cross, far]
    barrier = pltpu.get_barrier_semaphore()
    for peer in peers:
        pl.semaphore_signal(barrier, inc=1, device_id=peer, device_id_type=MESH)

    counts = {"remote": 0, "local": 0}
    started = []

    def send(src, dst, to):
        k = counts["remote"]
        counts["remote"] += 1
        copy = pltpu.make_async_remote_copy(
            src_ref=src, dst_ref=dst, send_sem=send_sem.at[k], recv_sem=recv_sem.at[k],
            device_id=to, device_id_type=MESH,
        )
        copy.start()
        started.append(copy)
        return copy

    def local(src, dst):
        k = counts["local"]
        counts["local"] += 1
        copy = pltpu.make_async_copy(src, dst, local_sem.at[k])
        copy.start()
        return copy

    def arrived(copies):
        for copy in copies:
            copy.wait_recv()

    def fill_edges(field, n):
        erow[n, 0] = field[1, 8:24, :]
        erow[n, 1] = field[8, 8:24, :]
        for i in range(ROWS):
            ecol[n, 0, i : i + 1, :] = field[i + 1, 8:9, :]
            ecol[n, 1, i : i + 1, :] = field[i + 1, 23:24, :]

    def send_edges(n):
        low, high = pl.ds(0, 8), pl.ds(8, 8)
        return [
            send(erow.at[n, 1], rrow.at[n, 0], at_grid(1, 0)),
            send(erow.at[n, 0], rrow.at[n, 1], at_grid(-1, 0)),
            send(ecol.at[n, 1], rcol.at[n, 0], at_grid(0, 1)),
            send(ecol.at[n, 0], rcol.at[n, 1], at_grid(0, -1)),
            send(erow.at[n, 1, high], rcor.at[n, 0], at_grid(1, 1)),
            send(erow.at[n, 1, low], rcor.at[n, 1], at_grid(1, -1)),
            send(erow.at[n, 0, high], rcor.at[n, 2], at_grid(-1, 1)),
            send(erow.at[n, 0, low], rcor.at[n, 3], at_grid(-1, -1)),
        ]

    one, zero = jnp.float32(1), jnp.float32(0)
    top = jnp.where(z > 0, one, zero)
    bottom = jnp.where(z < 3, one, zero)
    left = jnp.where(col > 0, one, zero)
    right = jnp.where(col < 7, one, zero)

    def fill_halo(field, n):
        field[0, 8:24, :] = rrow[n, 0] * top
        field[9, 8:24, :] = rrow[n, 1] * bottom
        for i in range(ROWS):
            field[i + 1, 7:8, :] = rcol[n, 0, i : i + 1, :] * left
            field[i + 1, 24:25, :] = rcol[n, 1, i : i + 1, :] * right
        field[0, 7:8, :] = rcor[n, 0, 7:8, :] * (top * left)
        field[0, 24:25, :] = rcor[n, 1, 0:1, :] * (top * right)
        field[9, 7:8, :] = rcor[n, 2, 7:8, :] * (bottom * left)
        field[9, 24:25, :] = rcor[n, 3, 0:1, :] * (bottom * right)

    shift = tp * 32
    frame = pl.ds(mul(tp * 768, 128), FR)
    filled = pl.ds(mul(tp * 32, 16), DQ)

    def to_frame(field, i, values):
        field[i + 1, 8:24, 768:896] = jnp.zeros((COLS, 128), F32)
        field[i + 1, 8:24, 0:DQ] = values.astype(F32)
        return pltpu.roll(field[i + 1, 8:24, :], shift, 1)

    for i in range(ROWS):
        padded[i + 1, 8:24, :] = to_frame(padded, i, tok_ref[i])
    fill_edges(padded, 0)
    pl.semaphore_wait(barrier, len(peers))
    halo = send_edges(0)
    for i in range(ROWS):
        cot[i * COLS : (i + 1) * COLS, :] = to_frame(padded2, i, cot_ref[i]).astype(BF16)

    def own_transpose(g, source):
        for k in range(7):
            trans[g, tp, k * 128 : k * 128 + 128, :] = source[:, k * 128 : k * 128 + 128].T

    def send_chunk(g, j, to):
        rows = pl.ds(mul(j * 32, 16), DQ)
        return send(trans.at[g, j, rows], trans.at[g, j, rows], to)

    own_transpose(0, cot)
    cot_cross = send_chunk(0, tp, cross)
    cot_sib = send_chunk(0, tp, sib)

    arrived(halo)
    fill_halo(padded, 0)

    def conv_row(i, squares):
        total = padded[i + 1, 8:24, :]
        for p in range(3):
            for q in range(3):
                total = total + pk_ref[p, q : q + 1, frame] * padded[i + p, 7 + q : 23 + q, :]
        rows = pl.ds(mul(i * COLS, 16), COLS)
        total = total.astype(BF16)
        pos[rows, :] = total
        total = total.astype(F32)
        b1[rows, 0:FR] = (total * gain_ref[0:1, frame]).astype(BF16)
        inv[rows, :] = jnp.broadcast_to(jnp.sum(total * total, axis=1, keepdims=True), (COLS, TOK))
        return squares

    lax.fori_loop(0, ROWS, conv_row, 0)
    own_transpose(1, b1)
    pos_cross = send_chunk(1, tp, cross)
    pos_sib = send_chunk(1, tp, sib)
    inn[0, tp] = inv[...].T[0:8, :]
    square_copies = [send(inn.at[0, tp], inn.at[0, tp], to) for to in (sib, cross, far)]

    def product_chunk(g, j, first):
        total, weight = (pre, w1) if g else (dact, w2)
        part = jnp.dot(weight[:, pl.ds(mul(j * 768, 128), FR)], trans[g, j], preferred_element_type=F32)
        total[...] = part if first else total[...] + part

    own_half = pl.ds(mul(core * HQ, 16), HQ)

    def lanes_of(z_index):
        return pl.ds(mul(z_index * TOK, 128), TOK)

    def half_of(j):
        return pl.ds(mul(j * 32 + core * HQ, 16), HQ)

    def spread_a(g):
        copies = []
        for d in (1, 2, 3):
            target = (z + d) % 4
            copies.append(
                send(trans.at[g, target, half_of(target)], at.at[g, y, own_half, lanes_of(z)], at_z(d))
            )
        return copies, local(trans.at[g, z, half_of(z)], at.at[g, y, own_half, lanes_of(z)])

    def spread_b(part):
        g, first, count = PARTS[part]
        copies = []
        for d in (1, 2, 3):
            rows = pl.ds(mul((y + d) % 4 * HQ + first, 16), count)
            copies.append(
                send(bt.at[g, rows], btile.at[g, y, pl.ds(first, count), lanes_of(z)], at_y(d))
            )
        rows = pl.ds(mul(y * HQ + first, 16), count)
        return copies, local(bt.at[g, rows], btile.at[g, y, pl.ds(first, count), lanes_of(z)])

    class Gather:
        def __init__(self, spread, block, piece, to, me, share):
            arrived(spread[0])
            spread[1].wait()
            self.block, self.piece, self.to, self.me, self.share = block, piece, to, me, share
            self.shared = []
            own = block(me)
            self.up, self.down = send(own, own, to(1)), send(own, own, to(3))
            self.to_sibling(own)

        def to_sibling(self, ref):
            if self.share:
                self.shared.append(send(ref, ref, sib))

        def forward(self):
            below, above = (self.me + 3) % 4, (self.me + 1) % 4
            self.up.wait_recv()
            first = self.piece(below, 0)
            self.up = send(first, first, self.to(1))
            self.down.wait_recv()
            second = self.piece(above, 1)
            self.down = send(second, second, self.to(3))
            self.to_sibling(self.block(below))
            self.to_sibling(self.block(above))

        def end(self):
            self.up.wait_recv()
            self.down.wait_recv()
            self.to_sibling(self.block((self.me + 2) % 4))

        def ready(self):
            arrived(self.shared)

    def gather_a(g, spread):
        def block(i):
            return at.at[g, i, own_half]

        def piece(i, h):
            return at.at[g, i, own_half, pl.ds(h * 256, 256)]

        return Gather(spread, block, piece, at_y, y, True)

    def gather_b(part, spread):
        g, first, count = PARTS[part]

        def block(i):
            return btile.at[g, :, pl.ds(first, count), lanes_of(i)]

        def piece(i, h):
            return btile.at[g, pl.ds(h * 2, 2), pl.ds(first, count), lanes_of(i)]

        return Gather(spread, block, piece, at_z, z, False)

    arrived([cot_cross])
    cot_far = send_chunk(0, tp_cross, sib)
    for copy in w_copies[:4]:
        copy.wait()
    product_chunk(0, tp, True)
    arrived([cot_sib])
    product_chunk(0, tp_sib, False)
    arrived([cot_far])
    spread_cot = spread_a(0)
    product_chunk(0, tp_cross, False)
    product_chunk(0, tp_far, False)
    for copy in w_copies[4:]:
        copy.wait()
    product_chunk(1, tp, True)
    arrived([pos_cross])
    pos_far = send_chunk(1, tp_cross, sib)
    arrived([pos_sib])
    product_chunk(1, tp_sib, False)
    product_chunk(1, tp_cross, False)
    gather_cot = gather_a(0, spread_cot)
    arrived([pos_far])
    spread_pos = spread_a(1)
    product_chunk(1, tp_far, False)
    arrived(square_copies)
    squares = inn[0, 0] + inn[0, 1] + inn[0, 2] + inn[0, 3]
    row_inv = lax.rsqrt(squares[0:1, :] * (1.0 / D) + epsilon)

    def gelu_tile(k, total):
        rows = pl.ds(mul(k * 64, 16), 64)
        raw = pre[rows, :]
        value = raw * row_inv
        cdf = 0.5 * (1.0 + lax.erf(value * 0.7071067811865476))
        density = jnp.exp(-0.5 * value * value) * 0.3989422804014327
        slope = (dact[rows, :] * (cdf + value * density) * row_inv).astype(BF16)
        bt[0, rows, :] = (value * cdf).astype(BF16)
        bt[1, rows, :] = slope
        return total + jnp.sum(slope.astype(F32) * raw, axis=0, keepdims=True)

    inner = lax.fori_loop(0, 25, gelu_tile, jnp.zeros((1, TOK), F32))
    spread_act = spread_b(0)
    inn[1, tp] = jnp.broadcast_to(inner, (8, TOK))
    inner_copies = [send(inn.at[1, tp], inn.at[1, tp], to) for to in (sib, cross, far)]

    for k in range(12):
        b1[:, k * 128 : k * 128 + 128] = bt[1, k * 128 : k * 128 + 128, :].T
    b1[:, 1536:1600] = bt[1, 1536:1600, :].T

    def norm_chunk(j):
        part = jnp.dot(b1[...], w1[:, pl.ds(mul(j * 768, 128), FR)], preferred_element_type=F32)
        return part.astype(BF16)

    e_copies = []
    for k, (j, to) in enumerate(((tp_far, far), (tp_cross, cross), (tp_sib, sib))):
        e_send[k] = norm_chunk(j)
        e_copies.append(send(e_send.at[k], e_recv.at[tp], to))
    e_recv[tp] = norm_chunk(tp)
    gather_act = gather_b(0, spread_act)
    spread_pre = [spread_b(1), spread_b(2)]
    gather_cot.forward()
    gather_pos = gather_a(1, spread_pos)

    arrived(inner_copies)
    arrived(e_copies)
    inner_row = inn[1, 0] + inn[1, 1] + inn[1, 2] + inn[1, 3]
    factor = inner_row[0:1, :] * row_inv * row_inv * (1.0 / D)
    inv[...] = jnp.broadcast_to(factor, (TOK, TOK)).T

    def hidden_row(i, total):
        rows = pl.ds(mul(i * COLS, 16), COLS)
        e = e_recv[0, rows, :].astype(F32) + e_recv[1, rows, :].astype(F32)
        e = e + e_recv[2, rows, :].astype(F32) + e_recv[3, rows, :].astype(F32)
        h = pos[rows, :].astype(F32)
        d = cot[rows, :].astype(F32) + gain_ref[0:1, frame] * e - h * inv[rows, 0:1]
        padded2[i + 1, 8:24, :] = d.astype(BF16).astype(F32)
        return total + e * h

    gain_sum = lax.fori_loop(0, ROWS, hidden_row, jnp.zeros((COLS, FR), F32))
    fill_edges(padded2, 1)
    halo2 = send_edges(1)
    gather_act.forward()
    gather_pre = [gather_b(1, spread_pre[0]), gather_b(2, spread_pre[1])]

    kall[0, y] = jnp.zeros((16, FR), F32)
    kall[0, y, 9:10, :] = jnp.sum(gain_sum, axis=0, keepdims=True)
    for n in range(7):
        lanes = slice(n * 128, n * 128 + 128)

        def taps(i, totals, lanes=lanes):
            d = padded2[i + 1, 8:24, lanes]
            return tuple(
                totals[p * 3 + q] + d * padded[i + p, 7 + q : 23 + q, lanes] for p in range(3) for q in range(3)
            )

        sums = lax.fori_loop(0, ROWS, taps, tuple(jnp.zeros((COLS, 128), F32) for _ in range(9)))
        for k in range(9):
            kall[0, y, k : k + 1, lanes] = jnp.sum(sums[k], axis=0, keepdims=True)
    k_copies = [send(kall.at[0, y], kall.at[0, y], at_y(d)) for d in (1, 2, 3)]

    arrived(halo2)
    fill_halo(padded2, 1)
    unshift = FR - shift

    def back_row(i, carry):
        total = padded2[i + 1, 8:24, :]
        for p in range(3):
            for q in range(3):
                total = total + pk_ref[p, q : q + 1, frame] * padded2[i + 2 - p, 9 - q : 25 - q, :]
        gt_ref[i] = pltpu.roll(total, unshift, 1)[:, 0:DQ].astype(BF16)
        return carry

    lax.fori_loop(0, ROWS, back_row, 0)
    arrived(k_copies)
    kall[1, z] = kall[0, 0] + kall[0, 1] + kall[0, 2] + kall[0, 3]
    k_copies = [send(kall.at[1, z], kall.at[1, z], at_z(d)) for d in (1, 2, 3)]

    s = float(TOK * 32) ** -0.5

    xs, xr, keep = (xs0, xs1, xs2), (xr0, xr1, xr2), (keep0, keep1, keep2)
    ys, yr = (ys0, ys1, ys2), (yr0, yr1, yr2)

    def half(part, which):
        g, first, count = PARTS[part]
        rows, hidden = pl.ds(mul(which * HQ, 16), HQ), pl.ds(first, count)
        total = lax.dot_general(at[g, 0, rows, :], btile[g, 0, hidden, :], NT, preferred_element_type=F32)
        for k in range(1, 4):
            total = total + lax.dot_general(
                at[g, k, rows, :], btile[g, k, hidden, :], NT, preferred_element_type=F32
            )
        return total * s

    def product(part):
        xs[part][...] = half(part, 1 - xh).astype(BF16)
        copy = send(xs[part], xr[part], x_peer)
        keep[part][...] = half(part, xh)
        return copy

    def turn(part, copy):
        copy.wait_recv()
        for k in range(4):
            rows = slice(k * 100, k * 100 + 100)
            ys[part][k, 0:100, :] = (keep[part][rows, :] + xr[part][rows, :].astype(F32)).astype(BF16)
        own = local(ys[part].at[y], yr[part].at[y])
        return [send(ys[part].at[(y + d) % 4], yr[part].at[y], at_y(d)) for d in (1, 3, 2)], own

    gather_cot.end()
    gather_act.end()
    gather_cot.ready()
    x_copy0 = product(0)
    gather_pos.forward()
    for gather in gather_pre:
        gather.forward()
    arrived(k_copies)
    kall[2, xh] = kall[1, 0] + kall[1, 1] + kall[1, 2] + kall[1, 3]
    k_copy = send(kall.at[2, xh], kall.at[2, xh], x_peer)
    turns = [turn(0, x_copy0)]
    gather_pos.end()
    arrived([k_copy])
    kg_ref[...] = pltpu.roll((kall[2, 0] + kall[2, 1]) * s, unshift, 1)
    gather_pos.ready()
    gather_pre[0].end()
    x_copy1 = product(1)
    gather_pre[1].end()
    x_copy2 = product(2)
    turns.append(turn(1, x_copy1))
    turns.append(turn(2, x_copy2))
    for copies, own in turns:
        arrived(copies)
        own.wait()
    for copy in started:
        copy.wait_send()


def finish(gt_in, part0, part1, part2, small, gt_ref, ge_ref, gr_ref, gk_ref, gg_ref):
    gt_ref[...] = gt_in[...]
    for (g, first, count), part in zip(PARTS, (part0, part1, part2)):
        out = ge_ref if g else gr_ref
        for k in range(4):
            out[:, k * HQ + first : k * HQ + first + count] = part[k, 0:100, :].astype(F32)
    for p in range(3):
        gk_ref[p] = small[3 * p : 3 * p + 3, 0:DQ]
    gg_ref[...] = small[9:10, 0:DQ]


def on_device(tokens, cotangent, expand_weight, reduce_weight, position_kernel, norm_gain):
    vmem = pl.BlockSpec(memory_space=pltpu.VMEM)
    hbm = pl.BlockSpec(memory_space=pl.ANY)
    f32, bf16 = (lambda *s: pltpu.VMEM(s, F32)), (lambda *s: pltpu.VMEM(s, BF16))
    gt, part0, part1, part2, small = pl.pallas_call(
        kernel,
        out_shape=(
            jax.ShapeDtypeStruct((ROWS, COLS, DQ), BF16),
            *[jax.ShapeDtypeStruct((4, 112, n), BF16) for _, _, n in PARTS],
            jax.ShapeDtypeStruct((16, FR), F32),
        ),
        in_specs=[vmem, vmem, hbm, hbm, vmem, vmem],
        out_specs=(vmem,) * 5,
        scratch_shapes=[
            bf16(HD, D), bf16(HD, D),
            f32(10, 32, FR), f32(10, 32, FR),
            bf16(TOK, FR), bf16(TOK, FR),
            bf16(2, 4, FR, TOK),
            f32(HD, TOK), f32(HD, TOK),
            f32(TOK, TOK),
            bf16(2, HD, TOK), bf16(TOK, HD),
            bf16(2, 4, DQ, 512), bf16(2, 4, HQ, 512),
            bf16(3, TOK, FR), bf16(4, TOK, FR),
            f32(2, 4, 8, TOK),
            f32(2, 2, 16, FR), f32(2, 2, 8, FR),
            f32(2, 2, 16, FR), f32(2, 2, 8, FR), f32(2, 4, 8, FR),
            *[bf16(HQ, n) for _, _, n in PARTS],
            *[bf16(HQ, n) for _, _, n in PARTS],
            *[f32(HQ, n) for _, _, n in PARTS],
            *[bf16(4, 112, n) for _, _, n in PARTS],
            f32(3, 4, 16, FR),
            pltpu.SemaphoreType.DMA((112,)), pltpu.SemaphoreType.DMA((112,)),
            pltpu.SemaphoreType.DMA((8,)), pltpu.SemaphoreType.DMA((8,)),
        ],
        compiler_params=pltpu.CompilerParams(
            collective_id=0, has_side_effects=True, vmem_limit_bytes=60 * 2**20
        ),
        name="mlp_backward",
    )(tokens, cotangent, expand_weight.T, reduce_weight.T, position_kernel, norm_gain.reshape(1, D))
    grad_tokens, grad_expand, grad_reduce, grad_kernel, grad_gain = pl.pallas_call(
        finish,
        out_shape=(
            jax.ShapeDtypeStruct((ROWS, COLS, DQ), BF16),
            jax.ShapeDtypeStruct((100, HD), F32),
            jax.ShapeDtypeStruct((100, HD), F32),
            jax.ShapeDtypeStruct((3, 3, DQ), F32),
            jax.ShapeDtypeStruct((1, DQ), F32),
        ),
        in_specs=[vmem] * 5,
        out_specs=(vmem,) * 5,
        name="finish",
    )(gt, part0, part1, part2, small)
    return grad_tokens, grad_expand, grad_reduce, grad_kernel, grad_gain.reshape(DQ)


def solution(mesh):
    placed = (P("row", "col", "tp"), P("row", "col", "tp"), P(None, "tp"), P(None, "tp"), P(), P())
    return jax.shard_map(
        on_device,
        mesh=mesh,
        in_specs=placed,
        out_specs=(
            P("row", "col", "tp"),
            P(("row", "col"), "tp"),
            P(("row", "col"), "tp"),
            P(None, None, "tp"),
            P("tp"),
        ),
        check_vma=False,
    )
```

```python
import jax
import jax.numpy as jnp
from jax import lax
from jax.experimental import pallas as pl
from jax.experimental.pallas import tpu as pltpu
from jax.sharding import PartitionSpec as P

MESH = pl.DeviceIdType.MESH
F32 = jnp.float32
BF16 = jnp.bfloat16
epsilon = 1e-06
ROWS, COLS, TOK = 8, 16, 128
DQ, D, FR = 800, 3200, 896
HD, HQ = 1600, 400
NT = (((1,), (1,)), ((), ()))
PARTS = ((0, 0, 400), (1, 0, 256), (1, 256, 144))


def mul(value, by):
    return pl.multiple_of(value, by)


def kernel(
    tok_ref, cot_ref, w1_hbm, w2_hbm, pk_ref, gain_ref,
    gt_ref, yr0, yr1, yr2, kg_ref,
    w1, w2, gain, padded, padded2, cot, pos, trans, pre, dact, inv, bt, b1, at, btile,
    e_send, e_recv, inn, erow, ecol, rrow, rcol, rcor,
    xs0, xs1, xs2, xr0, xr1, xr2, keep0, keep1, keep2, ys0, ys1, ys2, kall,
    send_sem, recv_sem, local_sem, wsem,
):
    z = lax.axis_index("row")
    col = lax.axis_index("col")
    tp = lax.axis_index("tp")
    xh, y = col // 4, col % 4
    xl, core = tp // 2, tp % 2

    def at_y(d):
        return (z, xh * 4 + (y + d) % 4, tp)

    def at_z(d):
        return ((z + d) % 4, col, tp)

    def at_grid(dr, dc):
        return ((z + dr + 4) % 4, (col + dc + 8) % 8, tp)

    x_peer = (z, (1 - xh) * 4 + y, tp)
    tp_sib = xl * 2 + 1 - core
    tp_cross = (1 - xl) * 2 + core
    tp_far = (1 - xl) * 2 + 1 - core
    sib, cross, far = (z, col, tp_sib), (z, col, tp_cross), (z, col, tp_far)

    w_copies = []
    for n, (src, dst) in enumerate(((w2_hbm, w2), (w1_hbm, w1))):
        for k in range(4):
            rows = pl.ds(k * HQ, HQ)
            copy = pltpu.make_async_copy(src.at[rows], dst.at[rows], wsem.at[n * 4 + k])
            copy.start()
            w_copies.append(copy)

    for k in range(25):
        gain[0:1, k * 128 : k * 128 + 128] = gain_ref[k : k + 1, :]

    for g in range(2):
        for j in range(4):
            trans[g, j, 0:96, :] = jnp.zeros((96, TOK), BF16)
            trans[g, j, 800:896, :] = jnp.zeros((96, TOK), BF16)

    grid_steps = [(1, 0), (-1, 0), (0, 1), (0, -1), (1, 1), (1, -1), (-1, 1), (-1, -1)]
    peers = [at_grid(*s) for s in grid_steps]
    peers += [at_y(d) for d in (1, 2, 3)] + [at_z(d) for d in (1, 2, 3)]
    peers += [x_peer, sib, cross, far]
    barrier = pltpu.get_barrier_semaphore()
    for peer in peers:
        pl.semaphore_signal(barrier, inc=1, device_id=peer, device_id_type=MESH)

    counts = {"remote": 0, "local": 0}
    started = []

    def send(src, dst, to):
        k = counts["remote"]
        counts["remote"] += 1
        copy = pltpu.make_async_remote_copy(
            src_ref=src, dst_ref=dst, send_sem=send_sem.at[k], recv_sem=recv_sem.at[k],
            device_id=to, device_id_type=MESH,
        )
        copy.start()
        started.append(copy)
        return copy

    def local(src, dst):
        k = counts["local"]
        counts["local"] += 1
        copy = pltpu.make_async_copy(src, dst, local_sem.at[k])
        copy.start()
        return copy

    def arrived(copies):
        for copy in copies:
            copy.wait_recv()

    def fill_edges(field, n):
        erow[n, 0] = field[1, 8:24, :]
        erow[n, 1] = field[8, 8:24, :]
        for i in range(ROWS):
            ecol[n, 0, i : i + 1, :] = field[i + 1, 8:9, :]
            ecol[n, 1, i : i + 1, :] = field[i + 1, 23:24, :]

    def send_edges(n):
        low, high = pl.ds(0, 8), pl.ds(8, 8)
        return [
            send(erow.at[n, 1], rrow.at[n, 0], at_grid(1, 0)),
            send(erow.at[n, 0], rrow.at[n, 1], at_grid(-1, 0)),
            send(ecol.at[n, 1], rcol.at[n, 0], at_grid(0, 1)),
            send(ecol.at[n, 0], rcol.at[n, 1], at_grid(0, -1)),
            send(erow.at[n, 1, high], rcor.at[n, 0], at_grid(1, 1)),
            send(erow.at[n, 1, low], rcor.at[n, 1], at_grid(1, -1)),
            send(erow.at[n, 0, high], rcor.at[n, 2], at_grid(-1, 1)),
            send(erow.at[n, 0, low], rcor.at[n, 3], at_grid(-1, -1)),
        ]

    one, zero = jnp.float32(1), jnp.float32(0)
    top = jnp.where(z > 0, one, zero)
    bottom = jnp.where(z < 3, one, zero)
    left = jnp.where(col > 0, one, zero)
    right = jnp.where(col < 7, one, zero)

    def fill_halo(field, n):
        field[0, 8:24, :] = rrow[n, 0] * top
        field[9, 8:24, :] = rrow[n, 1] * bottom
        for i in range(ROWS):
            field[i + 1, 7:8, :] = rcol[n, 0, i : i + 1, :] * left
            field[i + 1, 24:25, :] = rcol[n, 1, i : i + 1, :] * right
        field[0, 7:8, :] = rcor[n, 0, 7:8, :] * (top * left)
        field[0, 24:25, :] = rcor[n, 1, 0:1, :] * (top * right)
        field[9, 7:8, :] = rcor[n, 2, 7:8, :] * (bottom * left)
        field[9, 24:25, :] = rcor[n, 3, 0:1, :] * (bottom * right)

    shift = tp * 32
    frame = pl.ds(mul(tp * 768, 128), FR)
    filled = pl.ds(mul(tp * 32, 16), DQ)

    def to_frame(field, i, values):
        field[i + 1, 8:24, 768:896] = jnp.zeros((COLS, 128), F32)
        field[i + 1, 8:24, 0:DQ] = values.astype(F32)
        return pltpu.roll(field[i + 1, 8:24, :], shift, 1)

    for i in range(ROWS):
        padded[i + 1, 8:24, :] = to_frame(padded, i, tok_ref[i])
    fill_edges(padded, 0)
    pl.semaphore_wait(barrier, len(peers))
    halo = send_edges(0)
    for i in range(ROWS):
        cot[i * COLS : (i + 1) * COLS, :] = to_frame(padded2, i, cot_ref[i]).astype(BF16)

    def own_transpose(g, source):
        for k in range(7):
            trans[g, tp, k * 128 : k * 128 + 128, :] = source[:, k * 128 : k * 128 + 128].T

    def send_chunk(g, j, to):
        rows = pl.ds(mul(j * 32, 16), DQ)
        return send(trans.at[g, j, rows], trans.at[g, j, rows], to)

    own_transpose(0, cot)
    cot_cross = send_chunk(0, tp, cross)
    cot_sib = send_chunk(0, tp, sib)

    arrived(halo)
    fill_halo(padded, 0)

    def conv_row(i, squares):
        total = padded[i + 1, 8:24, :]
        for p in range(3):
            for q in range(3):
                total = total + pk_ref[p, q : q + 1, frame] * padded[i + p, 7 + q : 23 + q, :]
        rows = pl.ds(mul(i * COLS, 16), COLS)
        total = total.astype(BF16)
        pos[rows, :] = total
        total = total.astype(F32)
        b1[rows, 0:FR] = (total * gain[0:1, frame]).astype(BF16)
        inv[rows, :] = jnp.broadcast_to(jnp.sum(total * total, axis=1, keepdims=True), (COLS, TOK))
        return squares

    lax.fori_loop(0, ROWS, conv_row, 0)
    own_transpose(1, b1)
    pos_cross = send_chunk(1, tp, cross)
    pos_sib = send_chunk(1, tp, sib)
    inn[0, tp] = inv[...].T[0:8, :]
    square_copies = [send(inn.at[0, tp], inn.at[0, tp], to) for to in (sib, cross, far)]

    def product_chunk(g, j, first):
        total, weight = (pre, w1) if g else (dact, w2)
        part = jnp.dot(weight[:, pl.ds(mul(j * 768, 128), FR)], trans[g, j], preferred_element_type=F32)
        total[...] = part if first else total[...] + part

    own_half = pl.ds(mul(core * HQ, 16), HQ)

    def lanes_of(z_index):
        return pl.ds(mul(z_index * TOK, 128), TOK)

    def half_of(j):
        return pl.ds(mul(j * 32 + core * HQ, 16), HQ)

    def spread_a(g):
        copies = []
        for d in (1, 2, 3):
            target = (z + d) % 4
            copies.append(
                send(trans.at[g, target, half_of(target)], at.at[g, y, own_half, lanes_of(z)], at_z(d))
            )
        return copies, local(trans.at[g, z, half_of(z)], at.at[g, y, own_half, lanes_of(z)])

    def spread_b(part):
        g, first, count = PARTS[part]
        copies = []
        for d in (1, 2, 3):
            rows = pl.ds(mul((y + d) % 4 * HQ + first, 16), count)
            copies.append(
                send(bt.at[g, rows], btile.at[g, y, pl.ds(first, count), lanes_of(z)], at_y(d))
            )
        rows = pl.ds(mul(y * HQ + first, 16), count)
        return copies, local(bt.at[g, rows], btile.at[g, y, pl.ds(first, count), lanes_of(z)])

    class Gather:
        def __init__(self, spread, block, piece, to, me, share):
            arrived(spread[0])
            spread[1].wait()
            self.block, self.piece, self.to, self.me, self.share = block, piece, to, me, share
            self.shared = []
            own = block(me)
            self.up, self.down = send(own, own, to(1)), send(own, own, to(3))
            self.to_sibling(own)

        def to_sibling(self, ref):
            if self.share:
                self.shared.append(send(ref, ref, sib))

        def forward(self):
            below, above = (self.me + 3) % 4, (self.me + 1) % 4
            self.up.wait_recv()
            first = self.piece(below, 0)
            self.up = send(first, first, self.to(1))
            self.down.wait_recv()
            second = self.piece(above, 1)
            self.down = send(second, second, self.to(3))
            self.to_sibling(self.block(below))
            self.to_sibling(self.block(above))

        def end(self):
            self.up.wait_recv()
            self.down.wait_recv()
            self.to_sibling(self.block((self.me + 2) % 4))

        def ready(self):
            arrived(self.shared)

    def gather_a(g, spread):
        def block(i):
            return at.at[g, i, own_half]

        def piece(i, h):
            return at.at[g, i, own_half, pl.ds(h * 256, 256)]

        return Gather(spread, block, piece, at_y, y, True)

    def gather_b(part, spread):
        g, first, count = PARTS[part]

        def block(i):
            return btile.at[g, :, pl.ds(first, count), lanes_of(i)]

        def piece(i, h):
            return btile.at[g, pl.ds(h * 2, 2), pl.ds(first, count), lanes_of(i)]

        return Gather(spread, block, piece, at_z, z, False)

    arrived([cot_cross])
    cot_far = send_chunk(0, tp_cross, sib)
    for copy in w_copies[:4]:
        copy.wait()
    product_chunk(0, tp, True)
    arrived([cot_sib])
    product_chunk(0, tp_sib, False)
    arrived([cot_far])
    spread_cot = spread_a(0)
    product_chunk(0, tp_cross, False)
    product_chunk(0, tp_far, False)
    for copy in w_copies[4:]:
        copy.wait()
    product_chunk(1, tp, True)
    arrived([pos_cross])
    pos_far = send_chunk(1, tp_cross, sib)
    arrived([pos_sib])
    product_chunk(1, tp_sib, False)
    product_chunk(1, tp_cross, False)
    gather_cot = gather_a(0, spread_cot)
    arrived([pos_far])
    spread_pos = spread_a(1)
    product_chunk(1, tp_far, False)
    arrived(square_copies)
    squares = inn[0, 0] + inn[0, 1] + inn[0, 2] + inn[0, 3]
    row_inv = lax.rsqrt(squares[0:1, :] * (1.0 / D) + epsilon)

    def gelu_tile(k, total):
        rows = pl.ds(mul(k * 64, 16), 64)
        raw = pre[rows, :]
        value = raw * row_inv
        cdf = 0.5 * (1.0 + lax.erf(value * 0.7071067811865476))
        density = jnp.exp(-0.5 * value * value) * 0.3989422804014327
        slope = (dact[rows, :] * (cdf + value * density) * row_inv).astype(BF16)
        bt[0, rows, :] = (value * cdf).astype(BF16)
        bt[1, rows, :] = slope
        return total + jnp.sum(slope.astype(F32) * raw, axis=0, keepdims=True)

    inner = lax.fori_loop(0, 25, gelu_tile, jnp.zeros((1, TOK), F32))
    spread_act = spread_b(0)
    spread_pre = [spread_b(1), spread_b(2)]
    inn[1, tp] = jnp.broadcast_to(inner, (8, TOK))
    inner_copies = [send(inn.at[1, tp], inn.at[1, tp], to) for to in (sib, cross, far)]

    for k in range(12):
        b1[:, k * 128 : k * 128 + 128] = bt[1, k * 128 : k * 128 + 128, :].T
    b1[:, 1536:1600] = bt[1, 1536:1600, :].T

    def norm_chunk(j):
        part = jnp.dot(b1[...], w1[:, pl.ds(mul(j * 768, 128), FR)], preferred_element_type=F32)
        return part.astype(BF16)

    e_copies = []
    for k, (j, to) in enumerate(((tp_far, far), (tp_cross, cross), (tp_sib, sib))):
        e_send[k] = norm_chunk(j)
        e_copies.append(send(e_send.at[k], e_recv.at[tp], to))
    e_recv[tp] = norm_chunk(tp)
    gather_act = gather_b(0, spread_act)
    gather_cot.forward()
    gather_pos = gather_a(1, spread_pos)

    arrived(inner_copies)
    arrived(e_copies)
    inner_row = inn[1, 0] + inn[1, 1] + inn[1, 2] + inn[1, 3]
    factor = inner_row[0:1, :] * row_inv * row_inv * (1.0 / D)
    inv[...] = jnp.broadcast_to(factor, (TOK, TOK)).T

    def hidden_row(i, total):
        rows = pl.ds(mul(i * COLS, 16), COLS)
        e = e_recv[0, rows, :].astype(F32) + e_recv[1, rows, :].astype(F32)
        e = e + e_recv[2, rows, :].astype(F32) + e_recv[3, rows, :].astype(F32)
        h = pos[rows, :].astype(F32)
        d = cot[rows, :].astype(F32) + gain[0:1, frame] * e - h * inv[rows, 0:1]
        padded2[i + 1, 8:24, :] = d.astype(BF16).astype(F32)
        return total + e * h

    gain_sum = lax.fori_loop(0, ROWS, hidden_row, jnp.zeros((COLS, FR), F32))
    fill_edges(padded2, 1)
    halo2 = send_edges(1)
    gather_act.forward()
    gather_pre = [gather_b(1, spread_pre[0]), gather_b(2, spread_pre[1])]
    gather_cot.end()

    kall[0, y] = jnp.zeros((16, FR), F32)
    kall[0, y, 9:10, :] = jnp.sum(gain_sum, axis=0, keepdims=True)
    for n in range(7):
        lanes = slice(n * 128, n * 128 + 128)

        def taps(i, totals, lanes=lanes):
            d = padded2[i + 1, 8:24, lanes]
            return tuple(
                totals[p * 3 + q] + d * padded[i + p, 7 + q : 23 + q, lanes] for p in range(3) for q in range(3)
            )

        sums = lax.fori_loop(0, ROWS, taps, tuple(jnp.zeros((COLS, 128), F32) for _ in range(9)))
        for k in range(9):
            kall[0, y, k : k + 1, lanes] = jnp.sum(sums[k], axis=0, keepdims=True)
    k_copies = [send(kall.at[0, y], kall.at[0, y], at_y(d)) for d in (1, 2, 3)]

    gather_pos.forward()
    arrived(halo2)
    fill_halo(padded2, 1)
    unshift = FR - shift

    def back_row(i, carry):
        total = padded2[i + 1, 8:24, :]
        for p in range(3):
            for q in range(3):
                total = total + pk_ref[p, q : q + 1, frame] * padded2[i + 2 - p, 9 - q : 25 - q, :]
        gt_ref[i] = pltpu.roll(total, unshift, 1)[:, 0:DQ].astype(BF16)
        return carry

    lax.fori_loop(0, ROWS, back_row, 0)

    s = float(TOK * 32) ** -0.5

    xs, xr, keep = (xs0, xs1, xs2), (xr0, xr1, xr2), (keep0, keep1, keep2)
    ys, yr = (ys0, ys1, ys2), (yr0, yr1, yr2)

    def half(part, which):
        g, first, count = PARTS[part]
        rows, hidden = pl.ds(mul(which * HQ, 16), HQ), pl.ds(first, count)
        total = lax.dot_general(at[g, 0, rows, :], btile[g, 0, hidden, :], NT, preferred_element_type=F32)
        for k in range(1, 4):
            total = total + lax.dot_general(
                at[g, k, rows, :], btile[g, k, hidden, :], NT, preferred_element_type=F32
            )
        return total * s

    def product(part):
        xs[part][...] = half(part, 1 - xh).astype(BF16)
        copy = send(xs[part], xr[part], x_peer)
        keep[part][...] = half(part, xh)
        return copy

    def turn(part, copy):
        copy.wait_recv()
        for k in range(4):
            rows = slice(k * 100, k * 100 + 100)
            ys[part][k, 0:100, :] = (keep[part][rows, :] + xr[part][rows, :].astype(F32)).astype(BF16)
        own = local(ys[part].at[y], yr[part].at[y])
        return [send(ys[part].at[(y + d) % 4], yr[part].at[y], at_y(d)) for d in (1, 3, 2)], own

    gather_act.end()
    gather_cot.ready()
    x_copy0 = product(0)
    for gather in gather_pre:
        gather.forward()
    gather_pos.end()
    arrived(k_copies)
    kall[1, z] = kall[0, 0] + kall[0, 1] + kall[0, 2] + kall[0, 3]
    k_copies = [send(kall.at[1, z], kall.at[1, z], at_z(d)) for d in (1, 2, 3)]
    turns = [turn(0, x_copy0)]
    gather_pos.ready()
    gather_pre[0].end()
    x_copy1 = product(1)
    gather_pre[1].end()
    x_copy2 = product(2)
    arrived(k_copies)
    kall[2, xh] = kall[1, 0] + kall[1, 1] + kall[1, 2] + kall[1, 3]
    k_copy = send(kall.at[2, xh], kall.at[2, xh], x_peer)
    turns.append(turn(1, x_copy1))
    turns.append(turn(2, x_copy2))
    arrived([k_copy])
    kg_ref[...] = pltpu.roll((kall[2, 0] + kall[2, 1]) * s, unshift, 1)
    for copies, own in turns:
        arrived(copies)
        own.wait()
    for copy in started:
        copy.wait_send()


def finish(gt_in, part0, part1, part2, small, gt_ref, ge_ref, gr_ref, gk_ref, gg_ref):
    gt_ref[...] = gt_in[...]
    for (g, first, count), part in zip(PARTS, (part0, part1, part2)):
        out = ge_ref if g else gr_ref
        for k in range(4):
            out[:, k * HQ + first : k * HQ + first + count] = part[k, 0:100, :].astype(F32)
    for p in range(3):
        gk_ref[p] = small[3 * p : 3 * p + 3, 0:DQ]
    gg_ref[...] = small[9, 0:DQ]


def on_device(tokens, cotangent, expand_weight, reduce_weight, position_kernel, norm_gain):
    vmem = pl.BlockSpec(memory_space=pltpu.VMEM)
    hbm = pl.BlockSpec(memory_space=pl.ANY)
    f32, bf16 = (lambda *s: pltpu.VMEM(s, F32)), (lambda *s: pltpu.VMEM(s, BF16))
    gt, part0, part1, part2, small = pl.pallas_call(
        kernel,
        out_shape=(
            jax.ShapeDtypeStruct((ROWS, COLS, DQ), BF16),
            *[jax.ShapeDtypeStruct((4, 112, n), BF16) for _, _, n in PARTS],
            jax.ShapeDtypeStruct((16, FR), F32),
        ),
        in_specs=[vmem, vmem, hbm, hbm, vmem, vmem],
        out_specs=(vmem,) * 5,
        scratch_shapes=[
            bf16(HD, D), bf16(HD, D), f32(1, D),
            f32(10, 32, FR), f32(10, 32, FR),
            bf16(TOK, FR), bf16(TOK, FR),
            bf16(2, 4, FR, TOK),
            f32(HD, TOK), f32(HD, TOK),
            f32(TOK, TOK),
            bf16(2, HD, TOK), bf16(TOK, HD),
            bf16(2, 4, DQ, 512), bf16(2, 4, HQ, 512),
            bf16(3, TOK, FR), bf16(4, TOK, FR),
            f32(2, 4, 8, TOK),
            f32(2, 2, 16, FR), f32(2, 2, 8, FR),
            f32(2, 2, 16, FR), f32(2, 2, 8, FR), f32(2, 4, 8, FR),
            *[bf16(HQ, n) for _, _, n in PARTS],
            *[bf16(HQ, n) for _, _, n in PARTS],
            *[f32(HQ, n) for _, _, n in PARTS],
            *[bf16(4, 112, n) for _, _, n in PARTS],
            f32(3, 4, 16, FR),
            pltpu.SemaphoreType.DMA((112,)), pltpu.SemaphoreType.DMA((112,)),
            pltpu.SemaphoreType.DMA((8,)), pltpu.SemaphoreType.DMA((8,)),
        ],
        compiler_params=pltpu.CompilerParams(
            collective_id=0, has_side_effects=True, vmem_limit_bytes=60 * 2**20
        ),
        name="mlp_backward",
    )(tokens, cotangent, expand_weight.T, reduce_weight.T, position_kernel, norm_gain.reshape(25, 128))
    grad_tokens, grad_expand, grad_reduce, grad_kernel, grad_gain = pl.pallas_call(
        finish,
        out_shape=(
            jax.ShapeDtypeStruct((ROWS, COLS, DQ), BF16),
            jax.ShapeDtypeStruct((100, HD), F32),
            jax.ShapeDtypeStruct((100, HD), F32),
            jax.ShapeDtypeStruct((3, 3, DQ), F32),
            jax.ShapeDtypeStruct((DQ,), F32),
        ),
        in_specs=[vmem] * 5,
        out_specs=(vmem,) * 5,
        name="finish",
    )(gt, part0, part1, part2, small)
    return grad_tokens, grad_expand, grad_reduce, grad_kernel, grad_gain


def solution(mesh):
    placed = (P("row", "col", "tp"), P("row", "col", "tp"), P(None, "tp"), P(None, "tp"), P(), P())
    return jax.shard_map(
        on_device,
        mesh=mesh,
        in_specs=placed,
        out_specs=(
            P("row", "col", "tp"),
            P(("row", "col"), "tp"),
            P(("row", "col"), "tp"),
            P(None, None, "tp"),
            P("tp"),
        ),
        check_vma=False,
    )
```

```python
import jax
import jax.numpy as jnp
from jax import lax
from jax.experimental import pallas as pl
from jax.experimental.pallas import tpu as pltpu
from jax.sharding import PartitionSpec as P

MESH = pl.DeviceIdType.MESH
F32 = jnp.float32
BF16 = jnp.bfloat16
epsilon = 1e-06
ROWS, COLS, TOK = 8, 16, 128
DQ, D, FR = 800, 3200, 896
HD, HQ = 1600, 400
NT = (((1,), (1,)), ((), ()))
PARTS = ((0, 0, 400), (1, 0, 256), (1, 256, 144))


def mul(value, by):
    return pl.multiple_of(value, by)


def kernel(
    tok_ref, cot_ref, w1_hbm, w2_hbm, pk_ref, gain_ref,
    gt_ref, yr0, yr1, yr2, kg_ref,
    w1, w2, gain, padded, padded2, cot, pos, trans, pre, dact, inv, bt, b1, at, btile,
    e_send, e_recv, inn, erow, ecol, rrow, rcol, rcor,
    xs0, xs1, xs2, xr0, xr1, xr2, keep0, keep1, keep2, ys0, ys1, ys2, kall,
    send_sem, recv_sem, local_sem, wsem,
):
    z = lax.axis_index("row")
    col = lax.axis_index("col")
    tp = lax.axis_index("tp")
    xh, y = col // 4, col % 4
    xl, core = tp // 2, tp % 2

    def at_y(d):
        return (z, xh * 4 + (y + d) % 4, tp)

    def at_z(d):
        return ((z + d) % 4, col, tp)

    def at_grid(dr, dc):
        return ((z + dr + 4) % 4, (col + dc + 8) % 8, tp)

    x_peer = (z, (1 - xh) * 4 + y, tp)
    tp_sib = xl * 2 + 1 - core
    tp_cross = (1 - xl) * 2 + core
    tp_far = (1 - xl) * 2 + 1 - core
    sib, cross, far = (z, col, tp_sib), (z, col, tp_cross), (z, col, tp_far)

    w_copies = []
    for n, (src, dst) in enumerate(((w2_hbm, w2), (w1_hbm, w1))):
        for k in range(4):
            rows = pl.ds(k * HQ, HQ)
            copy = pltpu.make_async_copy(src.at[rows], dst.at[rows], wsem.at[n * 4 + k])
            copy.start()
            w_copies.append(copy)

    for k in range(25):
        gain[0:1, k * 128 : k * 128 + 128] = gain_ref[k : k + 1, :]

    for g in range(2):
        for j in range(4):
            trans[g, j, 0:96, :] = jnp.zeros((96, TOK), BF16)
            trans[g, j, 800:896, :] = jnp.zeros((96, TOK), BF16)

    grid_steps = [(1, 0), (-1, 0), (0, 1), (0, -1), (1, 1), (1, -1), (-1, 1), (-1, -1)]
    peers = [at_grid(*s) for s in grid_steps]
    peers += [at_y(d) for d in (1, 2, 3)] + [at_z(d) for d in (1, 2, 3)]
    peers += [x_peer, sib, cross, far]
    barrier = pltpu.get_barrier_semaphore()
    for peer in peers:
        pl.semaphore_signal(barrier, inc=1, device_id=peer, device_id_type=MESH)

    counts = {"remote": 0, "local": 0}
    started = []

    def send(src, dst, to):
        k = counts["remote"]
        counts["remote"] += 1
        copy = pltpu.make_async_remote_copy(
            src_ref=src, dst_ref=dst, send_sem=send_sem.at[k], recv_sem=recv_sem.at[k],
            device_id=to, device_id_type=MESH,
        )
        copy.start()
        started.append(copy)
        return copy

    def local(src, dst):
        k = counts["local"]
        counts["local"] += 1
        copy = pltpu.make_async_copy(src, dst, local_sem.at[k])
        copy.start()
        return copy

    def arrived(copies):
        for copy in copies:
            copy.wait_recv()

    def fill_edges(field, n):
        erow[n, 0] = field[1, 8:24, :]
        erow[n, 1] = field[8, 8:24, :]
        for i in range(ROWS):
            ecol[n, 0, i : i + 1, :] = field[i + 1, 8:9, :]
            ecol[n, 1, i : i + 1, :] = field[i + 1, 23:24, :]

    def send_edges(n):
        low, high = pl.ds(0, 8), pl.ds(8, 8)
        return [
            send(erow.at[n, 1], rrow.at[n, 0], at_grid(1, 0)),
            send(erow.at[n, 0], rrow.at[n, 1], at_grid(-1, 0)),
            send(ecol.at[n, 1], rcol.at[n, 0], at_grid(0, 1)),
            send(ecol.at[n, 0], rcol.at[n, 1], at_grid(0, -1)),
            send(erow.at[n, 1, high], rcor.at[n, 0], at_grid(1, 1)),
            send(erow.at[n, 1, low], rcor.at[n, 1], at_grid(1, -1)),
            send(erow.at[n, 0, high], rcor.at[n, 2], at_grid(-1, 1)),
            send(erow.at[n, 0, low], rcor.at[n, 3], at_grid(-1, -1)),
        ]

    one, zero = jnp.float32(1), jnp.float32(0)
    top = jnp.where(z > 0, one, zero)
    bottom = jnp.where(z < 3, one, zero)
    left = jnp.where(col > 0, one, zero)
    right = jnp.where(col < 7, one, zero)

    def fill_halo(field, n):
        field[0, 8:24, :] = rrow[n, 0] * top
        field[9, 8:24, :] = rrow[n, 1] * bottom
        for i in range(ROWS):
            field[i + 1, 7:8, :] = rcol[n, 0, i : i + 1, :] * left
            field[i + 1, 24:25, :] = rcol[n, 1, i : i + 1, :] * right
        field[0, 7:8, :] = rcor[n, 0, 7:8, :] * (top * left)
        field[0, 24:25, :] = rcor[n, 1, 0:1, :] * (top * right)
        field[9, 7:8, :] = rcor[n, 2, 7:8, :] * (bottom * left)
        field[9, 24:25, :] = rcor[n, 3, 0:1, :] * (bottom * right)

    shift = tp * 32
    frame = pl.ds(mul(tp * 768, 128), FR)
    filled = pl.ds(mul(tp * 32, 16), DQ)

    def to_frame(field, i, values):
        field[i + 1, 8:24, 768:896] = jnp.zeros((COLS, 128), F32)
        field[i + 1, 8:24, 0:DQ] = values.astype(F32)
        return pltpu.roll(field[i + 1, 8:24, :], shift, 1)

    for i in range(ROWS):
        padded[i + 1, 8:24, :] = to_frame(padded, i, tok_ref[i])
    fill_edges(padded, 0)
    pl.semaphore_wait(barrier, len(peers))
    halo = send_edges(0)
    for i in range(ROWS):
        cot[i * COLS : (i + 1) * COLS, :] = to_frame(padded2, i, cot_ref[i]).astype(BF16)

    def own_transpose(g, source):
        for k in range(7):
            trans[g, tp, k * 128 : k * 128 + 128, :] = source[:, k * 128 : k * 128 + 128].T

    def send_chunk(g, j, to):
        rows = pl.ds(mul(j * 32, 16), DQ)
        return send(trans.at[g, j, rows], trans.at[g, j, rows], to)

    own_transpose(0, cot)
    cot_cross = send_chunk(0, tp, cross)
    cot_sib = send_chunk(0, tp, sib)

    arrived(halo)
    fill_halo(padded, 0)

    def conv_row(i, squares):
        total = padded[i + 1, 8:24, :]
        for p in range(3):
            for q in range(3):
                total = total + pk_ref[p, q : q + 1, frame] * padded[i + p, 7 + q : 23 + q, :]
        rows = pl.ds(mul(i * COLS, 16), COLS)
        total = total.astype(BF16)
        pos[rows, :] = total
        total = total.astype(F32)
        b1[rows, 0:FR] = (total * gain[0:1, frame]).astype(BF16)
        inv[rows, :] = jnp.broadcast_to(jnp.sum(total * total, axis=1, keepdims=True), (COLS, TOK))
        return squares

    lax.fori_loop(0, ROWS, conv_row, 0)
    own_transpose(1, b1)
    pos_cross = send_chunk(1, tp, cross)
    pos_sib = send_chunk(1, tp, sib)
    inn[0, tp] = inv[...].T[0:8, :]
    square_copies = [send(inn.at[0, tp], inn.at[0, tp], to) for to in (sib, cross, far)]

    def product_chunk(g, j, first):
        total, weight = (pre, w1) if g else (dact, w2)
        part = jnp.dot(weight[:, pl.ds(mul(j * 768, 128), FR)], trans[g, j], preferred_element_type=F32)
        total[...] = part if first else total[...] + part

    own_half = pl.ds(mul(core * HQ, 16), HQ)

    def lanes_of(z_index):
        return pl.ds(mul(z_index * TOK, 128), TOK)

    def half_of(j):
        return pl.ds(mul(j * 32 + core * HQ, 16), HQ)

    def spread_a(g):
        copies = []
        for d in (1, 2, 3):
            target = (z + d) % 4
            copies.append(
                send(trans.at[g, target, half_of(target)], at.at[g, y, own_half, lanes_of(z)], at_z(d))
            )
        return copies, local(trans.at[g, z, half_of(z)], at.at[g, y, own_half, lanes_of(z)])

    def spread_b(part):
        g, first, count = PARTS[part]
        copies = []
        for d in (1, 2, 3):
            rows = pl.ds(mul((y + d) % 4 * HQ + first, 16), count)
            copies.append(
                send(bt.at[g, rows], btile.at[g, y, pl.ds(first, count), lanes_of(z)], at_y(d))
            )
        rows = pl.ds(mul(y * HQ + first, 16), count)
        return copies, local(bt.at[g, rows], btile.at[g, y, pl.ds(first, count), lanes_of(z)])

    class Gather:
        def __init__(self, spread, block, piece, to, me, share):
            arrived(spread[0])
            spread[1].wait()
            self.block, self.piece, self.to, self.me, self.share = block, piece, to, me, share
            self.shared = []
            own = block(me)
            self.up, self.down = send(own, own, to(1)), send(own, own, to(3))
            self.to_sibling(own)

        def to_sibling(self, ref):
            if self.share:
                self.shared.append(send(ref, ref, sib))

        def forward(self):
            below, above = (self.me + 3) % 4, (self.me + 1) % 4
            self.up.wait_recv()
            first = self.piece(below, 0)
            self.up = send(first, first, self.to(1))
            self.down.wait_recv()
            second = self.piece(above, 1)
            self.down = send(second, second, self.to(3))
            self.to_sibling(self.block(below))
            self.to_sibling(self.block(above))

        def end(self):
            self.up.wait_recv()
            self.down.wait_recv()
            self.to_sibling(self.block((self.me + 2) % 4))

        def ready(self):
            arrived(self.shared)

    def gather_a(g, spread):
        def block(i):
            return at.at[g, i, own_half]

        def piece(i, h):
            return at.at[g, i, own_half, pl.ds(h * 256, 256)]

        return Gather(spread, block, piece, at_y, y, True)

    def gather_b(part, spread):
        g, first, count = PARTS[part]

        def block(i):
            return btile.at[g, :, pl.ds(first, count), lanes_of(i)]

        def piece(i, h):
            return btile.at[g, pl.ds(h * 2, 2), pl.ds(first, count), lanes_of(i)]

        return Gather(spread, block, piece, at_z, z, False)

    arrived([cot_cross])
    cot_far = send_chunk(0, tp_cross, sib)
    for copy in w_copies[:4]:
        copy.wait()
    product_chunk(0, tp, True)
    arrived([cot_sib])
    product_chunk(0, tp_sib, False)
    arrived([cot_far])
    spread_cot = spread_a(0)
    product_chunk(0, tp_cross, False)
    product_chunk(0, tp_far, False)
    for copy in w_copies[4:]:
        copy.wait()
    product_chunk(1, tp, True)
    arrived([pos_cross])
    pos_far = send_chunk(1, tp_cross, sib)
    arrived([pos_sib])
    product_chunk(1, tp_sib, False)
    product_chunk(1, tp_cross, False)
    gather_cot = gather_a(0, spread_cot)
    arrived([pos_far])
    spread_pos = spread_a(1)
    product_chunk(1, tp_far, False)
    arrived(square_copies)
    squares = inn[0, 0] + inn[0, 1] + inn[0, 2] + inn[0, 3]
    row_inv = lax.rsqrt(squares[0:1, :] * (1.0 / D) + epsilon)

    def gelu_tile(k, total):
        rows = pl.ds(mul(k * 64, 16), 64)
        raw = pre[rows, :]
        value = raw * row_inv
        cdf = 0.5 * (1.0 + lax.erf(value * 0.7071067811865476))
        density = jnp.exp(-0.5 * value * value) * 0.3989422804014327
        slope = (dact[rows, :] * (cdf + value * density) * row_inv).astype(BF16)
        bt[0, rows, :] = (value * cdf).astype(BF16)
        bt[1, rows, :] = slope
        return total + jnp.sum(slope.astype(F32) * raw, axis=0, keepdims=True)

    inner = lax.fori_loop(0, 25, gelu_tile, jnp.zeros((1, TOK), F32))
    spread_act = spread_b(0)
    inn[1, tp] = jnp.broadcast_to(inner, (8, TOK))
    inner_copies = [send(inn.at[1, tp], inn.at[1, tp], to) for to in (sib, cross, far)]

    s = float(TOK * 32) ** -0.5

    xs, xr, keep = (xs0, xs1, xs2), (xr0, xr1, xr2), (keep0, keep1, keep2)
    ys, yr = (ys0, ys1, ys2), (yr0, yr1, yr2)

    def half(part, which):
        g, first, count = PARTS[part]
        rows, hidden = pl.ds(mul(which * HQ, 16), HQ), pl.ds(first, count)
        total = lax.dot_general(at[g, 0, rows, :], btile[g, 0, hidden, :], NT, preferred_element_type=F32)
        for k in range(1, 4):
            total = total + lax.dot_general(
                at[g, k, rows, :], btile[g, k, hidden, :], NT, preferred_element_type=F32
            )
        return total * s

    def product(part):
        xs[part][...] = half(part, 1 - xh).astype(BF16)
        return send(xs[part], xr[part], x_peer)

    def product_own(part):
        keep[part][...] = half(part, xh)

    def turn(part, copy):
        copy.wait_recv()
        for k in range(4):
            rows = slice(k * 100, k * 100 + 100)
            ys[part][k, 0:100, :] = (keep[part][rows, :] + xr[part][rows, :].astype(F32)).astype(BF16)
        own = local(ys[part].at[y], yr[part].at[y])
        return [send(ys[part].at[(y + d) % 4], yr[part].at[y], at_y(d)) for d in (1, 3, 2)], own


    for k in range(12):
        b1[:, k * 128 : k * 128 + 128] = bt[1, k * 128 : k * 128 + 128, :].T
    b1[:, 1536:1600] = bt[1, 1536:1600, :].T

    def norm_chunk(j):
        part = jnp.dot(b1[...], w1[:, pl.ds(mul(j * 768, 128), FR)], preferred_element_type=F32)
        return part.astype(BF16)

    e_copies = []
    for k, (j, to) in enumerate(((tp_far, far), (tp_cross, cross), (tp_sib, sib))):
        e_send[k] = norm_chunk(j)
        e_copies.append(send(e_send.at[k], e_recv.at[tp], to))
    e_recv[tp] = norm_chunk(tp)
    gather_act = gather_b(0, spread_act)
    spread_pre = [spread_b(1), spread_b(2)]
    gather_cot.forward()

    arrived(inner_copies)
    arrived(e_copies)
    inner_row = inn[1, 0] + inn[1, 1] + inn[1, 2] + inn[1, 3]
    factor = inner_row[0:1, :] * row_inv * row_inv * (1.0 / D)
    inv[...] = jnp.broadcast_to(factor, (TOK, TOK)).T

    def hidden_row(i, total):
        rows = pl.ds(mul(i * COLS, 16), COLS)
        e = e_recv[0, rows, :].astype(F32) + e_recv[1, rows, :].astype(F32)
        e = e + e_recv[2, rows, :].astype(F32) + e_recv[3, rows, :].astype(F32)
        h = pos[rows, :].astype(F32)
        d = cot[rows, :].astype(F32) + gain[0:1, frame] * e - h * inv[rows, 0:1]
        padded2[i + 1, 8:24, :] = d.astype(BF16).astype(F32)
        return total + e * h

    gather_pos = gather_a(1, spread_pos)
    gain_sum = lax.fori_loop(0, ROWS, hidden_row, jnp.zeros((COLS, FR), F32))
    fill_edges(padded2, 1)
    halo2 = send_edges(1)
    gather_act.forward()
    gather_pre = [gather_b(1, spread_pre[0]), gather_b(2, spread_pre[1])]
    gather_cot.end()

    kall[0, y] = jnp.zeros((16, FR), F32)
    kall[0, y, 9:10, :] = jnp.sum(gain_sum, axis=0, keepdims=True)
    for n in range(7):
        lanes = slice(n * 128, n * 128 + 128)

        def taps(i, totals, lanes=lanes):
            d = padded2[i + 1, 8:24, lanes]
            return tuple(
                totals[p * 3 + q] + d * padded[i + p, 7 + q : 23 + q, lanes] for p in range(3) for q in range(3)
            )

        sums = lax.fori_loop(0, ROWS, taps, tuple(jnp.zeros((COLS, 128), F32) for _ in range(9)))
        for k in range(9):
            kall[0, y, k : k + 1, lanes] = jnp.sum(sums[k], axis=0, keepdims=True)
    k_copies = [send(kall.at[0, y], kall.at[0, y], at_y(d)) for d in (1, 2, 3)]

    gather_pos.forward()
    gather_act.end()
    gather_cot.ready()
    x_copy0 = product(0)
    product_own(0)
    arrived(halo2)
    fill_halo(padded2, 1)
    unshift = FR - shift

    def back_row(i, carry):
        total = padded2[i + 1, 8:24, :]
        for p in range(3):
            for q in range(3):
                total = total + pk_ref[p, q : q + 1, frame] * padded2[i + 2 - p, 9 - q : 25 - q, :]
        gt_ref[i] = pltpu.roll(total, unshift, 1)[:, 0:DQ].astype(BF16)
        return carry

    lax.fori_loop(0, ROWS, back_row, 0)

    for gather in gather_pre:
        gather.forward()
    gather_pos.end()
    arrived(k_copies)
    kall[1, z] = kall[0, 0] + kall[0, 1] + kall[0, 2] + kall[0, 3]
    k_copies = [send(kall.at[1, z], kall.at[1, z], at_z(d)) for d in (1, 2, 3)]
    turns = [turn(0, x_copy0)]
    gather_pos.ready()
    gather_pre[0].end()
    x_copy1 = product(1)
    gather_pre[1].end()
    x_copy2 = product(2)
    product_own(1)
    product_own(2)
    arrived(k_copies)
    kall[2, xh] = kall[1, 0] + kall[1, 1] + kall[1, 2] + kall[1, 3]
    k_copy = send(kall.at[2, xh], kall.at[2, xh], x_peer)
    turns.append(turn(1, x_copy1))
    turns.append(turn(2, x_copy2))
    arrived([k_copy])
    kg_ref[...] = pltpu.roll((kall[2, 0] + kall[2, 1]) * s, unshift, 1)
    for copies, own in turns:
        arrived(copies)
        own.wait()
    for copy in started:
        copy.wait_send()


def finish(gt_in, part0, part1, part2, small, gt_ref, ge_ref, gr_ref, gk_ref, gg_ref):
    gt_ref[...] = gt_in[...]
    for (g, first, count), part in zip(PARTS, (part0, part1, part2)):
        out = ge_ref if g else gr_ref
        for k in range(4):
            out[:, k * HQ + first : k * HQ + first + count] = part[k, 0:100, :].astype(F32)
    for p in range(3):
        gk_ref[p] = small[3 * p : 3 * p + 3, 0:DQ]
    gg_ref[...] = small[9, 0:DQ]


def on_device(tokens, cotangent, expand_weight, reduce_weight, position_kernel, norm_gain):
    vmem = pl.BlockSpec(memory_space=pltpu.VMEM)
    hbm = pl.BlockSpec(memory_space=pl.ANY)
    f32, bf16 = (lambda *s: pltpu.VMEM(s, F32)), (lambda *s: pltpu.VMEM(s, BF16))
    gt, part0, part1, part2, small = pl.pallas_call(
        kernel,
        out_shape=(
            jax.ShapeDtypeStruct((ROWS, COLS, DQ), BF16),
            *[jax.ShapeDtypeStruct((4, 112, n), BF16) for _, _, n in PARTS],
            jax.ShapeDtypeStruct((16, FR), F32),
        ),
        in_specs=[vmem, vmem, hbm, hbm, vmem, vmem],
        out_specs=(vmem,) * 5,
        scratch_shapes=[
            bf16(HD, D), bf16(HD, D), f32(1, D),
            f32(10, 32, FR), f32(10, 32, FR),
            bf16(TOK, FR), bf16(TOK, FR),
            bf16(2, 4, FR, TOK),
            f32(HD, TOK), f32(HD, TOK),
            f32(TOK, TOK),
            bf16(2, HD, TOK), bf16(TOK, HD),
            bf16(2, 4, DQ, 512), bf16(2, 4, HQ, 512),
            bf16(3, TOK, FR), bf16(4, TOK, FR),
            f32(2, 4, 8, TOK),
            f32(2, 2, 16, FR), f32(2, 2, 8, FR),
            f32(2, 2, 16, FR), f32(2, 2, 8, FR), f32(2, 4, 8, FR),
            *[bf16(HQ, n) for _, _, n in PARTS],
            *[bf16(HQ, n) for _, _, n in PARTS],
            *[f32(HQ, n) for _, _, n in PARTS],
            *[bf16(4, 112, n) for _, _, n in PARTS],
            f32(3, 4, 16, FR),
            pltpu.SemaphoreType.DMA((112,)), pltpu.SemaphoreType.DMA((112,)),
            pltpu.SemaphoreType.DMA((8,)), pltpu.SemaphoreType.DMA((8,)),
        ],
        compiler_params=pltpu.CompilerParams(
            collective_id=0, has_side_effects=True, vmem_limit_bytes=60 * 2**20
        ),
        name="mlp_backward",
    )(tokens, cotangent, expand_weight.T, reduce_weight.T, position_kernel, norm_gain.reshape(25, 128))
    grad_tokens, grad_expand, grad_reduce, grad_kernel, grad_gain = pl.pallas_call(
        finish,
        out_shape=(
            jax.ShapeDtypeStruct((ROWS, COLS, DQ), BF16),
            jax.ShapeDtypeStruct((100, HD), F32),
            jax.ShapeDtypeStruct((100, HD), F32),
            jax.ShapeDtypeStruct((3, 3, DQ), F32),
            jax.ShapeDtypeStruct((DQ,), F32),
        ),
        in_specs=[vmem] * 5,
        out_specs=(vmem,) * 5,
        name="finish",
    )(gt, part0, part1, part2, small)
    return grad_tokens, grad_expand, grad_reduce, grad_kernel, grad_gain


def solution(mesh):
    placed = (P("row", "col", "tp"), P("row", "col", "tp"), P(None, "tp"), P(None, "tp"), P(), P())
    return jax.shard_map(
        on_device,
        mesh=mesh,
        in_specs=placed,
        out_specs=(
            P("row", "col", "tp"),
            P(("row", "col"), "tp"),
            P(("row", "col"), "tp"),
            P(None, None, "tp"),
            P("tp"),
        ),
        check_vma=False,
    )
```

```python
import jax
import jax.numpy as jnp
from jax import lax
from jax.experimental import pallas as pl
from jax.experimental.pallas import tpu as pltpu
from jax.sharding import PartitionSpec as P

MESH = pl.DeviceIdType.MESH
F32 = jnp.float32
BF16 = jnp.bfloat16
epsilon = 1e-06
ROWS, COLS, TOK = 8, 16, 128
DQ, D, FR = 800, 3200, 896
HD, HQ = 1600, 400
NT = (((1,), (1,)), ((), ()))
PARTS = ((0, 0, 400), (1, 0, 256), (1, 256, 144))


def mul(value, by):
    return pl.multiple_of(value, by)


def kernel(
    tok_ref, cot_ref, w1_hbm, w2_hbm, pk_ref, gain_ref,
    gt_ref, yr0, yr1, yr2, kg_ref,
    w1, w2, gain, padded, padded2, cot, pos, trans, pre, dact, inv, bt, b1, at, btile,
    e_send, e_recv, inn, erow, ecol, rrow, rcol, rcor,
    xs0, xs1, xs2, xr0, xr1, xr2, keep0, keep1, keep2, ys0, ys1, ys2, kall,
    send_sem, recv_sem, local_sem, wsem,
):
    z = lax.axis_index("row")
    col = lax.axis_index("col")
    tp = lax.axis_index("tp")
    xh, y = col // 4, col % 4
    xl, core = tp // 2, tp % 2

    def at_y(d):
        return (z, xh * 4 + (y + d) % 4, tp)

    def at_z(d):
        return ((z + d) % 4, col, tp)

    def at_grid(dr, dc):
        return ((z + dr + 4) % 4, (col + dc + 8) % 8, tp)

    x_peer = (z, (1 - xh) * 4 + y, tp)
    tp_sib = xl * 2 + 1 - core
    tp_cross = (1 - xl) * 2 + core
    tp_far = (1 - xl) * 2 + 1 - core
    sib, cross, far = (z, col, tp_sib), (z, col, tp_cross), (z, col, tp_far)

    w_copies = []
    for n, (src, dst) in enumerate(((w2_hbm, w2), (w1_hbm, w1))):
        for k in range(4):
            rows = pl.ds(k * HQ, HQ)
            copy = pltpu.make_async_copy(src.at[rows], dst.at[rows], wsem.at[n * 4 + k])
            copy.start()
            w_copies.append(copy)

    for k in range(25):
        gain[0:1, k * 128 : k * 128 + 128] = gain_ref[k : k + 1, :]

    for g in range(2):
        for j in range(4):
            trans[g, j, 0:96, :] = jnp.zeros((96, TOK), BF16)
            trans[g, j, 800:896, :] = jnp.zeros((96, TOK), BF16)

    grid_steps = [(1, 0), (-1, 0), (0, 1), (0, -1), (1, 1), (1, -1), (-1, 1), (-1, -1)]
    peers = [at_grid(*s) for s in grid_steps]
    peers += [at_y(d) for d in (1, 2, 3)] + [at_z(d) for d in (1, 2, 3)]
    peers += [x_peer, sib, cross, far]
    barrier = pltpu.get_barrier_semaphore()
    for peer in peers:
        pl.semaphore_signal(barrier, inc=1, device_id=peer, device_id_type=MESH)

    counts = {"remote": 0, "local": 0}
    started = []

    def send(src, dst, to):
        k = counts["remote"]
        counts["remote"] += 1
        copy = pltpu.make_async_remote_copy(
            src_ref=src, dst_ref=dst, send_sem=send_sem.at[k], recv_sem=recv_sem.at[k],
            device_id=to, device_id_type=MESH,
        )
        copy.start()
        started.append(copy)
        return copy

    def local(src, dst):
        k = counts["local"]
        counts["local"] += 1
        copy = pltpu.make_async_copy(src, dst, local_sem.at[k])
        copy.start()
        return copy

    def arrived(copies):
        for copy in copies:
            copy.wait_recv()

    def fill_edges(field, n):
        erow[n, 0] = field[1, 8:24, :]
        erow[n, 1] = field[8, 8:24, :]
        for i in range(ROWS):
            ecol[n, 0, i : i + 1, :] = field[i + 1, 8:9, :]
            ecol[n, 1, i : i + 1, :] = field[i + 1, 23:24, :]

    def send_edges(n):
        low, high = pl.ds(0, 8), pl.ds(8, 8)
        return [
            send(erow.at[n, 1], rrow.at[n, 0], at_grid(1, 0)),
            send(erow.at[n, 0], rrow.at[n, 1], at_grid(-1, 0)),
            send(ecol.at[n, 1], rcol.at[n, 0], at_grid(0, 1)),
            send(ecol.at[n, 0], rcol.at[n, 1], at_grid(0, -1)),
            send(erow.at[n, 1, high], rcor.at[n, 0], at_grid(1, 1)),
            send(erow.at[n, 1, low], rcor.at[n, 1], at_grid(1, -1)),
            send(erow.at[n, 0, high], rcor.at[n, 2], at_grid(-1, 1)),
            send(erow.at[n, 0, low], rcor.at[n, 3], at_grid(-1, -1)),
        ]

    one, zero = jnp.float32(1), jnp.float32(0)
    top = jnp.where(z > 0, one, zero)
    bottom = jnp.where(z < 3, one, zero)
    left = jnp.where(col > 0, one, zero)
    right = jnp.where(col < 7, one, zero)

    def fill_halo(field, n):
        field[0, 8:24, :] = rrow[n, 0] * top
        field[9, 8:24, :] = rrow[n, 1] * bottom
        for i in range(ROWS):
            field[i + 1, 7:8, :] = rcol[n, 0, i : i + 1, :] * left
            field[i + 1, 24:25, :] = rcol[n, 1, i : i + 1, :] * right
        field[0, 7:8, :] = rcor[n, 0, 7:8, :] * (top * left)
        field[0, 24:25, :] = rcor[n, 1, 0:1, :] * (top * right)
        field[9, 7:8, :] = rcor[n, 2, 7:8, :] * (bottom * left)
        field[9, 24:25, :] = rcor[n, 3, 0:1, :] * (bottom * right)

    shift = tp * 32
    frame = pl.ds(mul(tp * 768, 128), FR)
    filled = pl.ds(mul(tp * 32, 16), DQ)

    def to_frame(field, i, values):
        field[i + 1, 8:24, 768:896] = jnp.zeros((COLS, 128), F32)
        field[i + 1, 8:24, 0:DQ] = values.astype(F32)
        return pltpu.roll(field[i + 1, 8:24, :], shift, 1)

    for i in range(ROWS):
        padded[i + 1, 8:24, :] = to_frame(padded, i, tok_ref[i])
    fill_edges(padded, 0)
    pl.semaphore_wait(barrier, len(peers))
    halo = send_edges(0)
    for i in range(ROWS):
        cot[i * COLS : (i + 1) * COLS, :] = to_frame(padded2, i, cot_ref[i]).astype(BF16)

    def own_transpose(g, source):
        for k in range(7):
            trans[g, tp, k * 128 : k * 128 + 128, :] = source[:, k * 128 : k * 128 + 128].T

    def send_chunk(g, j, to):
        rows = pl.ds(mul(j * 32, 16), DQ)
        return send(trans.at[g, j, rows], trans.at[g, j, rows], to)

    own_transpose(0, cot)
    cot_cross = send_chunk(0, tp, cross)
    cot_sib = send_chunk(0, tp, sib)

    arrived(halo)
    fill_halo(padded, 0)

    def conv_row(i, squares):
        total = padded[i + 1, 8:24, :]
        for p in range(3):
            for q in range(3):
                total = total + pk_ref[p, q : q + 1, frame] * padded[i + p, 7 + q : 23 + q, :]
        rows = pl.ds(mul(i * COLS, 16), COLS)
        total = total.astype(BF16)
        pos[rows, :] = total
        total = total.astype(F32)
        b1[rows, 0:FR] = (total * gain[0:1, frame]).astype(BF16)
        inv[rows, :] = jnp.broadcast_to(jnp.sum(total * total, axis=1, keepdims=True), (COLS, TOK))
        return squares

    lax.fori_loop(0, ROWS, conv_row, 0)
    own_transpose(1, b1)
    pos_cross = send_chunk(1, tp, cross)
    pos_sib = send_chunk(1, tp, sib)
    inn[0, tp] = inv[...].T[0:8, :]
    square_copies = [send(inn.at[0, tp], inn.at[0, tp], to) for to in (sib, cross, far)]

    def product_chunk(g, j, first):
        total, weight = (pre, w1) if g else (dact, w2)
        part = jnp.dot(weight[:, pl.ds(mul(j * 768, 128), FR)], trans[g, j], preferred_element_type=F32)
        total[...] = part if first else total[...] + part

    own_half = pl.ds(mul(core * HQ, 16), HQ)

    def lanes_of(z_index):
        return pl.ds(mul(z_index * TOK, 128), TOK)

    def half_of(j):
        return pl.ds(mul(j * 32 + core * HQ, 16), HQ)

    def spread_a(g):
        copies = []
        for d in (1, 2, 3):
            target = (z + d) % 4
            copies.append(
                send(trans.at[g, target, half_of(target)], at.at[g, y, own_half, lanes_of(z)], at_z(d))
            )
        return copies, local(trans.at[g, z, half_of(z)], at.at[g, y, own_half, lanes_of(z)])

    def spread_b(part):
        g, first, count = PARTS[part]
        copies = []
        for d in (1, 2, 3):
            rows = pl.ds(mul((y + d) % 4 * HQ + first, 16), count)
            copies.append(
                send(bt.at[g, rows], btile.at[g, y, pl.ds(first, count), lanes_of(z)], at_y(d))
            )
        rows = pl.ds(mul(y * HQ + first, 16), count)
        return copies, local(bt.at[g, rows], btile.at[g, y, pl.ds(first, count), lanes_of(z)])

    class Gather:
        def __init__(self, spread, block, piece, to, me, share):
            arrived(spread[0])
            spread[1].wait()
            self.block, self.piece, self.to, self.me, self.share = block, piece, to, me, share
            self.shared = []
            own = block(me)
            self.up, self.down = send(own, own, to(1)), send(own, own, to(3))
            self.to_sibling(own)

        def to_sibling(self, ref):
            if self.share:
                self.shared.append(send(ref, ref, sib))

        def forward(self):
            below, above = (self.me + 3) % 4, (self.me + 1) % 4
            self.up.wait_recv()
            first = self.piece(below, 0)
            self.up = send(first, first, self.to(1))
            self.to_sibling(self.block(below))
            self.down.wait_recv()
            second = self.piece(above, 1)
            self.down = send(second, second, self.to(3))
            self.to_sibling(self.block(above))

        def end(self):
            self.up.wait_recv()
            self.down.wait_recv()
            self.to_sibling(self.block((self.me + 2) % 4))

        def ready(self):
            arrived(self.shared)

    def gather_a(g, spread):
        def block(i):
            return at.at[g, i, own_half]

        def piece(i, h):
            return at.at[g, i, own_half, pl.ds(h * 256, 256)]

        return Gather(spread, block, piece, at_y, y, True)

    def gather_b(part, spread):
        g, first, count = PARTS[part]

        def block(i):
            return btile.at[g, :, pl.ds(first, count), lanes_of(i)]

        def piece(i, h):
            return btile.at[g, pl.ds(h * 2, 2), pl.ds(first, count), lanes_of(i)]

        return Gather(spread, block, piece, at_z, z, False)

    arrived([cot_cross])
    cot_far = send_chunk(0, tp_cross, sib)
    for copy in w_copies[:4]:
        copy.wait()
    product_chunk(0, tp, True)
    arrived([cot_sib])
    product_chunk(0, tp_sib, False)
    arrived([cot_far])
    spread_cot = spread_a(0)
    product_chunk(0, tp_cross, False)
    product_chunk(0, tp_far, False)
    for copy in w_copies[4:]:
        copy.wait()
    product_chunk(1, tp, True)
    arrived([pos_cross])
    pos_far = send_chunk(1, tp_cross, sib)
    arrived([pos_sib])
    product_chunk(1, tp_sib, False)
    product_chunk(1, tp_cross, False)
    gather_cot = gather_a(0, spread_cot)
    arrived([pos_far])
    spread_pos = spread_a(1)
    product_chunk(1, tp_far, False)
    arrived(square_copies)
    squares = inn[0, 0] + inn[0, 1] + inn[0, 2] + inn[0, 3]
    row_inv = lax.rsqrt(squares[0:1, :] * (1.0 / D) + epsilon)

    def gelu_tile(k, total):
        rows = pl.ds(mul(k * 64, 16), 64)
        raw = pre[rows, :]
        value = raw * row_inv
        cdf = 0.5 * (1.0 + lax.erf(value * 0.7071067811865476))
        density = jnp.exp(-0.5 * value * value) * 0.3989422804014327
        slope = (dact[rows, :] * (cdf + value * density) * row_inv).astype(BF16)
        bt[0, rows, :] = (value * cdf).astype(BF16)
        bt[1, rows, :] = slope
        return total + jnp.sum(slope.astype(F32) * raw, axis=0, keepdims=True)

    inner = lax.fori_loop(0, 25, gelu_tile, jnp.zeros((1, TOK), F32))
    spread_act = spread_b(0)
    inn[1, tp] = jnp.broadcast_to(inner, (8, TOK))
    inner_copies = [send(inn.at[1, tp], inn.at[1, tp], to) for to in (sib, cross, far)]

    s = float(TOK * 32) ** -0.5

    xs, xr, keep = (xs0, xs1, xs2), (xr0, xr1, xr2), (keep0, keep1, keep2)
    ys, yr = (ys0, ys1, ys2), (yr0, yr1, yr2)

    def half(part, which):
        g, first, count = PARTS[part]
        rows, hidden = pl.ds(mul(which * HQ, 16), HQ), pl.ds(first, count)
        total = lax.dot_general(at[g, 0, rows, :], btile[g, 0, hidden, :], NT, preferred_element_type=F32)
        for k in range(1, 4):
            total = total + lax.dot_general(
                at[g, k, rows, :], btile[g, k, hidden, :], NT, preferred_element_type=F32
            )
        return total * s

    def product(part):
        xs[part][...] = half(part, 1 - xh).astype(BF16)
        return send(xs[part], xr[part], x_peer)

    def product_own(part):
        keep[part][...] = half(part, xh)

    def turn(part, copy):
        copy.wait_recv()
        for k in range(4):
            rows = slice(k * 100, k * 100 + 100)
            ys[part][k, 0:100, :] = (keep[part][rows, :] + xr[part][rows, :].astype(F32)).astype(BF16)
        own = local(ys[part].at[y], yr[part].at[y])
        return [send(ys[part].at[(y + d) % 4], yr[part].at[y], at_y(d)) for d in (1, 3, 2)], own


    for k in range(12):
        b1[:, k * 128 : k * 128 + 128] = bt[1, k * 128 : k * 128 + 128, :].T
    b1[:, 1536:1600] = bt[1, 1536:1600, :].T

    def norm_chunk(j):
        part = jnp.dot(b1[...], w1[:, pl.ds(mul(j * 768, 128), FR)], preferred_element_type=F32)
        return part.astype(BF16)

    e_copies = []
    for k, (j, to) in enumerate(((tp_far, far), (tp_cross, cross), (tp_sib, sib))):
        e_send[k] = norm_chunk(j)
        e_copies.append(send(e_send.at[k], e_recv.at[tp], to))
    e_recv[tp] = norm_chunk(tp)
    gather_act = gather_b(0, spread_act)
    spread_pre = [spread_b(1), spread_b(2)]
    gather_cot.forward()

    arrived(inner_copies)
    arrived(e_copies)
    inner_row = inn[1, 0] + inn[1, 1] + inn[1, 2] + inn[1, 3]
    factor = inner_row[0:1, :] * row_inv * row_inv * (1.0 / D)
    inv[...] = jnp.broadcast_to(factor, (TOK, TOK)).T

    def hidden_row(i, total):
        rows = pl.ds(mul(i * COLS, 16), COLS)
        e = e_recv[0, rows, :].astype(F32) + e_recv[1, rows, :].astype(F32)
        e = e + e_recv[2, rows, :].astype(F32) + e_recv[3, rows, :].astype(F32)
        h = pos[rows, :].astype(F32)
        d = cot[rows, :].astype(F32) + gain[0:1, frame] * e - h * inv[rows, 0:1]
        padded2[i + 1, 8:24, :] = d.astype(BF16).astype(F32)
        return total + e * h

    gather_pos = gather_a(1, spread_pos)
    gain_sum = lax.fori_loop(0, ROWS, hidden_row, jnp.zeros((COLS, FR), F32))
    fill_edges(padded2, 1)
    halo2 = send_edges(1)
    gather_act.forward()
    gather_pre = [gather_b(1, spread_pre[0]), gather_b(2, spread_pre[1])]
    gather_cot.end()

    kall[0, y] = jnp.zeros((16, FR), F32)
    kall[0, y, 9:10, :] = jnp.sum(gain_sum, axis=0, keepdims=True)
    for n in range(7):
        lanes = slice(n * 128, n * 128 + 128)

        def taps(i, totals, lanes=lanes):
            d = padded2[i + 1, 8:24, lanes]
            return tuple(
                totals[p * 3 + q] + d * padded[i + p, 7 + q : 23 + q, lanes] for p in range(3) for q in range(3)
            )

        sums = lax.fori_loop(0, ROWS, taps, tuple(jnp.zeros((COLS, 128), F32) for _ in range(9)))
        for k in range(9):
            kall[0, y, k : k + 1, lanes] = jnp.sum(sums[k], axis=0, keepdims=True)
    k_copies = [send(kall.at[0, y], kall.at[0, y], at_y(d)) for d in (1, 2, 3)]

    gather_pos.forward()
    gather_act.end()
    gather_cot.ready()
    x_copy0 = product(0)
    product_own(0)
    arrived(halo2)
    fill_halo(padded2, 1)
    unshift = FR - shift

    def back_row(i, carry):
        total = padded2[i + 1, 8:24, :]
        for p in range(3):
            for q in range(3):
                total = total + pk_ref[p, q : q + 1, frame] * padded2[i + 2 - p, 9 - q : 25 - q, :]
        gt_ref[i] = pltpu.roll(total, unshift, 1)[:, 0:DQ].astype(BF16)
        return carry

    lax.fori_loop(0, ROWS, back_row, 0)

    for gather in gather_pre:
        gather.forward()
    gather_pos.end()
    arrived(k_copies)
    kall[1, z] = kall[0, 0] + kall[0, 1] + kall[0, 2] + kall[0, 3]
    k_copies = [send(kall.at[1, z], kall.at[1, z], at_z(d)) for d in (1, 2, 3)]
    turns = [turn(0, x_copy0)]
    gather_pos.ready()
    gather_pre[0].end()
    x_copy1 = product(1)
    gather_pre[1].end()
    x_copy2 = product(2)
    product_own(1)
    product_own(2)
    arrived(k_copies)
    kall[2, xh] = kall[1, 0] + kall[1, 1] + kall[1, 2] + kall[1, 3]
    k_copy = send(kall.at[2, xh], kall.at[2, xh], x_peer)
    turns.append(turn(1, x_copy1))
    turns.append(turn(2, x_copy2))
    arrived([k_copy])
    kg_ref[...] = pltpu.roll((kall[2, 0] + kall[2, 1]) * s, unshift, 1)
    for copies, own in turns:
        arrived(copies)
        own.wait()
    for copy in started:
        copy.wait_send()


def finish(gt_in, part0, part1, part2, small, gt_ref, ge_ref, gr_ref, gk_ref, gg_ref):
    gt_ref[...] = gt_in[...]
    for (g, first, count), part in zip(PARTS, (part0, part1, part2)):
        out = ge_ref if g else gr_ref
        for k in range(4):
            out[:, k * HQ + first : k * HQ + first + count] = part[k, 0:100, :].astype(F32)
    for p in range(3):
        gk_ref[p] = small[3 * p : 3 * p + 3, 0:DQ]
    gg_ref[...] = small[9, 0:DQ]


def on_device(tokens, cotangent, expand_weight, reduce_weight, position_kernel, norm_gain):
    vmem = pl.BlockSpec(memory_space=pltpu.VMEM)
    hbm = pl.BlockSpec(memory_space=pl.ANY)
    f32, bf16 = (lambda *s: pltpu.VMEM(s, F32)), (lambda *s: pltpu.VMEM(s, BF16))
    gt, part0, part1, part2, small = pl.pallas_call(
        kernel,
        out_shape=(
            jax.ShapeDtypeStruct((ROWS, COLS, DQ), BF16),
            *[jax.ShapeDtypeStruct((4, 112, n), BF16) for _, _, n in PARTS],
            jax.ShapeDtypeStruct((16, FR), F32),
        ),
        in_specs=[vmem, vmem, hbm, hbm, vmem, vmem],
        out_specs=(vmem,) * 5,
        scratch_shapes=[
            bf16(HD, D), bf16(HD, D), f32(1, D),
            f32(10, 32, FR), f32(10, 32, FR),
            bf16(TOK, FR), bf16(TOK, FR),
            bf16(2, 4, FR, TOK),
            f32(HD, TOK), f32(HD, TOK),
            f32(TOK, TOK),
            bf16(2, HD, TOK), bf16(TOK, HD),
            bf16(2, 4, DQ, 512), bf16(2, 4, HQ, 512),
            bf16(3, TOK, FR), bf16(4, TOK, FR),
            f32(2, 4, 8, TOK),
            f32(2, 2, 16, FR), f32(2, 2, 8, FR),
            f32(2, 2, 16, FR), f32(2, 2, 8, FR), f32(2, 4, 8, FR),
            *[bf16(HQ, n) for _, _, n in PARTS],
            *[bf16(HQ, n) for _, _, n in PARTS],
            *[f32(HQ, n) for _, _, n in PARTS],
            *[bf16(4, 112, n) for _, _, n in PARTS],
            f32(3, 4, 16, FR),
            pltpu.SemaphoreType.DMA((112,)), pltpu.SemaphoreType.DMA((112,)),
            pltpu.SemaphoreType.DMA((8,)), pltpu.SemaphoreType.DMA((8,)),
        ],
        compiler_params=pltpu.CompilerParams(
            collective_id=0, has_side_effects=True, vmem_limit_bytes=60 * 2**20
        ),
        name="mlp_backward",
    )(tokens, cotangent, expand_weight.T, reduce_weight.T, position_kernel, norm_gain.reshape(25, 128))
    grad_tokens, grad_expand, grad_reduce, grad_kernel, grad_gain = pl.pallas_call(
        finish,
        out_shape=(
            jax.ShapeDtypeStruct((ROWS, COLS, DQ), BF16),
            jax.ShapeDtypeStruct((100, HD), F32),
            jax.ShapeDtypeStruct((100, HD), F32),
            jax.ShapeDtypeStruct((3, 3, DQ), F32),
            jax.ShapeDtypeStruct((DQ,), F32),
        ),
        in_specs=[vmem] * 5,
        out_specs=(vmem,) * 5,
        name="finish",
    )(gt, part0, part1, part2, small)
    return grad_tokens, grad_expand, grad_reduce, grad_kernel, grad_gain


def solution(mesh):
    placed = (P("row", "col", "tp"), P("row", "col", "tp"), P(None, "tp"), P(None, "tp"), P(), P())
    return jax.shard_map(
        on_device,
        mesh=mesh,
        in_specs=placed,
        out_specs=(
            P("row", "col", "tp"),
            P(("row", "col"), "tp"),
            P(("row", "col"), "tp"),
            P(None, None, "tp"),
            P("tp"),
        ),
        check_vma=False,
    )
```
